32 devices in a mesh: win: 2 (over y), chan: 16 (over z, x, core).
Axes of the slice: x: 2, y: 2, z: 4, core: 2. Of those that a mesh axis runs over, the one named last changes fastest.
Arguments:
- strain_raw: bfloat16 [256, 4352], P('chan', 'win'), may hold values from -6 to 6
- fir_taps: bfloat16 [128], replicated, may hold values from -0.5 to 0.5
- live_mask: int32 [256], P('chan'), may hold values 0 or 1
- window_start: int32 [8], P('win'), may hold values from 0 to 132
Outputs:
- stack: float32 [128, 101, 256], P('chan', None, 'win')
The draws below stay inside these ranges and needn't reach their ends.
All inputs are finite; a program needn't handle non-finite values. No bound on the sum of `live_mask` on one device may be relied on, other than what follows from the above.
Results may differ from the reference program's by a relative error of at most 0.0018.
Values may be sent and summed in bfloat16 or wider, within the bound.
A program may use at most 128 MiB of HBM per device.

```python
import math
import jax
import jax.numpy as jnp
from jax import lax

CH_DEV = 16
NS = 1024
DECIM = 4
TAPS = 128
HALF = 32
LAGS = 101
STRIDE = 2
SPAN = 4220
RECORD = 4352
WINDOWS = 8
CHANNELS = 256
NSRC = 128


def touch_ends(values, stream_key, least, top_value):
    spot = [jax.random.randint(jax.random.fold_in(stream_key, axis), (), 0, length) for axis, length in enumerate(values.shape)]
    longest = values.shape.index(max(values.shape))
    beside = spot[:longest] + [(spot[longest] + 1) % values.shape[longest]] + spot[longest + 1:]
    return values.at[tuple(spot)].set(least).at[tuple(beside)].set(top_value)


def level_of(own_key, shape, pieces, smallest, largest):
    def one(axis_at, parts):
        draws = jax.random.uniform(jax.random.fold_in(jax.random.fold_in(own_key, 6), axis_at), (parts,), jnp.float32, smallest / len(pieces), largest / len(pieces))
        return jnp.repeat(jnp.exp(draws), shape[axis_at] // parts).reshape((-1,) + (1,) * (len(shape) - axis_at - 1))

    level = one(*pieces[0])
    for cut in pieces[1:]:
        level = level * one(*cut)
    return level


def bell_draw(key, extent, spread, limit, cuts=(), kind=jnp.bfloat16):
    values = jax.random.normal(key, extent, jnp.float32) * spread
    if len(cuts) > 0:
        values = level_of(key, extent, cuts, -0.22, 0.18) * values
    return jnp.clip(values, min=-limit, max=limit).astype(kind)


def setup_inputs(seed: int = 0) -> dict:
    arg_keys = jax.random.split(jax.random.key(seed), 5)
    strain_raw = bell_draw(arg_keys[0], (CHANNELS, RECORD), 1.0, 6.0, ((0, 16), (1, 2)))
    fir_taps = bell_draw(arg_keys[1], (TAPS,), TAPS ** -0.5, 0.5)
    live_mask = touch_ends((jax.random.randint(arg_keys[2], (CHANNELS,), 0, 8) < 7).astype(jnp.int32), jax.random.fold_in(arg_keys[2], 1), 0, 1)
    window_start = touch_ends(jax.random.randint(arg_keys[3], (WINDOWS,), 0, RECORD - SPAN + 1), jax.random.fold_in(arg_keys[3], 1), 0, RECORD - SPAN).astype(jnp.int32)
    return dict(strain_raw=strain_raw, fir_taps=fir_taps, live_mask=live_mask, window_start=window_start)


EPSILON = 1e-06

def smooth_circular(amplitude):
    padded = jnp.concatenate([amplitude[:, NS - HALF:], amplitude, amplitude[:, :HALF]], axis=1)
    summed = lax.reduce_window(padded, jnp.array(0, padded.dtype), lax.add, (1, 2 * HALF + 1), (1, 1), 'VALID')
    return summed / (2 * HALF + 1)

def whiten_window(strain_raw, fir_taps, live_mask, start_at):
    window = lax.dynamic_slice_in_dim(strain_raw, start_at, SPAN, 1).astype(jnp.float32)
    taps_wide = fir_taps.astype(jnp.float32)
    decimated = jnp.zeros((strain_raw.shape[0], NS), jnp.float32)
    for tap_at in range(TAPS):
        decimated = decimated + taps_wide[tap_at] * window[:, tap_at:tap_at + (NS - 1) * DECIM + 1:DECIM]
    spectrum = jnp.fft.fft(decimated, axis=1)
    real_part = jnp.real(spectrum)
    imag_part = jnp.imag(spectrum)
    amplitude = jnp.sqrt(real_part * real_part + imag_part * imag_part)
    smooth = smooth_circular(amplitude)
    flattened = spectrum / (smooth + EPSILON)
    series = jnp.real(jnp.fft.ifft(flattened, axis=1)) * jnp.sqrt(jnp.float32(NS))
    series = series * live_mask.astype(jnp.float32)[:, None]
    return series.astype(jnp.bfloat16)

def reference(strain_raw, fir_taps, live_mask, window_start):

    def one_window(start_at):
        return whiten_window(strain_raw, fir_taps, live_mask, start_at)
    whitened = lax.map(one_window, window_start)
    spectra = jnp.fft.fft(whitened.astype(jnp.float32), axis=2)
    conjugate = jnp.conj(spectra)
    source_ids = jnp.arange(NSRC)
    owners = source_ids // CH_DEV * (STRIDE * CH_DEV) + source_ids % CH_DEV
    source_spectra = spectra[:, owners]
    block_size = math.gcd(NSRC, 8)
    blocks = source_spectra.reshape(WINDOWS, NSRC // block_size, block_size, NS).transpose(1, 0, 2, 3)
    lag_pick = (jnp.arange(LAGS) - LAGS // 2) % NS

    def one_block(block):
        cross = jnp.einsum('wcf,wsf->scf', conjugate, block)
        lagged = jnp.real(jnp.fft.ifft(cross, axis=2))[:, :, lag_pick]
        return jnp.transpose(lagged, (0, 2, 1))
    summed = lax.map(one_block, blocks).reshape(NSRC, LAGS, CHANNELS)
    return (summed / jnp.sqrt(jnp.float32(NS) * WINDOWS)).astype(jnp.float32)
```

```python
import math

import jax
import jax.numpy as jnp
import ml_dtypes
import numpy as np
from jax import lax
from jax.experimental import pallas as pl
from jax.experimental.pallas import tpu as pltpu
from jax.sharding import PartitionSpec as P

NS = 1024
DECIM = 4
TAPS = 128
HALF = 32
LAGS = 101
STRIDE = 2
EPSILON = 1e-06

FOLD = NS // 2
BLOCK = 128
REACH = BLOCK * DECIM + TAPS
LAG_ROWS = 112
VMEM_LIMIT = 48 * 1024 * 1024


def split_table(table):
    high = table.astype(ml_dtypes.bfloat16)
    low = (table - high.astype(np.float64)).astype(ml_dtypes.bfloat16)
    return high, low


def build_tables():
    time_at = np.arange(FOLD)
    forward = []
    inverse = []
    for parity in range(2):
        bins = 2 * np.arange(NS // 4) + parity
        angle = 2.0 * np.pi * ((time_at[:, None] * bins[None, :]) % NS) / NS
        cosine = np.cos(angle)
        sine = -np.sin(angle)
        weight = np.full((2 * bins.size,), 2.0 / math.sqrt(NS))
        if parity == 0:
            sine[:, 0] = np.cos(np.pi * time_at)
            weight[0] = 1.0 / math.sqrt(NS)
            weight[bins.size] = 1.0 / math.sqrt(NS)
        table = np.concatenate([cosine, sine], axis=1)
        forward.append(table)
        inverse.append((table * weight[None, :]).T)
    order = np.concatenate([np.arange(0, FOLD, 2), np.arange(1, FOLD, 2), [FOLD]])
    place = np.zeros((FOLD + 1,), np.int64)
    place[order] = np.arange(FOLD + 1)
    counts = np.zeros((FOLD + 1, FOLD + 1))
    for column, bin_at in enumerate(order):
        for offset in range(-HALF, HALF + 1):
            seen = (bin_at + offset) % NS
            counts[place[min(seen, NS - seen)], column] += 1.0
    mean_table = counts[:FOLD, :FOLD].astype(ml_dtypes.bfloat16)
    edge = np.zeros((8, FOLD), np.float32)
    edge[0] = counts[FOLD, :FOLD]
    edge[1] = counts[:FOLD, FOLD]
    forward_high, forward_low = split_table(np.stack(forward))
    inverse_high, inverse_low = split_table(np.stack(inverse))
    return forward_high, forward_low, inverse_high, inverse_low, mean_table, edge


def dot(left, right):
    return jnp.dot(left, right, preferred_element_type=jnp.float32)


def split_dot(value, high, low):
    rows = value.shape[0]
    value_high = value.astype(jnp.bfloat16)
    value_low = (value - value_high.astype(jnp.float32)).astype(jnp.bfloat16)
    both = dot(jnp.concatenate([value_high, value_low], axis=0), high)
    return both[:rows] + both[rows:] + dot(value_high, low)


def whiten_kernel(windows, starts, record, band, forward_high, forward_low, inverse_high, inverse_low,
                  mean_table, edge, live, out):
    channels, length = record.shape
    wide = record[...].astype(jnp.float32)
    pieces = []
    for window_at in range(windows):
        start = starts[window_at]
        rolled = pltpu.roll(wide, lax.rem(length - start, length), 1).astype(jnp.bfloat16)
        parts = [
            dot(rolled[:, at * BLOCK * DECIM : at * BLOCK * DECIM + REACH], band[...])
            for at in range(NS // BLOCK)
        ]
        pieces.append(jnp.concatenate(parts, axis=1))
    decimated = jnp.concatenate(pieces, axis=0)
    first, second = decimated[:, :FOLD], decimated[:, FOLD:]
    even = split_dot(first + second, forward_high[0], forward_low[0])
    odd = split_dot(first - second, forward_high[1], forward_low[1])
    quarter = NS // 4
    real_part = jnp.concatenate([even[:, :quarter], odd[:, :quarter]], axis=1)
    imag_part = jnp.concatenate([even[:, quarter:], odd[:, quarter:]], axis=1)
    at_zero = lax.broadcasted_iota(jnp.int32, real_part.shape, 1) == 0
    amplitude = jnp.sqrt(real_part * real_part + jnp.where(at_zero, 0.0, imag_part * imag_part))
    top = jnp.abs(imag_part[:, 0:1])
    amp_high = amplitude.astype(jnp.bfloat16)
    amp_low = (amplitude - amp_high.astype(jnp.float32)).astype(jnp.bfloat16)
    summed = dot(amp_high, mean_table[...]) + dot(amp_low, mean_table[...]) + top * edge[0:1, :]
    summed_top = jnp.sum(amplitude * edge[1:2, :], axis=1, keepdims=True) + top
    width = 2 * HALF + 1
    scale = 1.0 / (summed * (1.0 / width) + EPSILON)
    scale_top = 1.0 / (summed_top * (1.0 / width) + EPSILON)
    white_real = real_part * scale
    white_imag = imag_part * jnp.where(at_zero, scale_top, scale)
    white_even = jnp.concatenate([white_real[:, :quarter], white_imag[:, :quarter]], axis=1)
    white_odd = jnp.concatenate([white_real[:, quarter:], white_imag[:, quarter:]], axis=1)
    from_even = split_dot(white_even, inverse_high[0], inverse_low[0])
    from_odd = split_dot(white_odd, inverse_high[1], inverse_low[1])
    series = jnp.concatenate([from_even + from_odd, from_even - from_odd], axis=1)
    for window_at in range(windows):
        rows = series[window_at * channels : (window_at + 1) * channels]
        out[window_at] = (rows * live[...]).astype(jnp.bfloat16)


def lag_sums(place, gathered, turned, lagged):
    blocks, windows, channels, _ = gathered.shape
    sources = channels // STRIDE
    chan_at = place[1]
    source_block = chan_at // STRIDE * STRIDE
    source_part = lax.rem(chan_at, STRIDE)
    total = None
    for window_at in range(windows):
        rows = gathered[source_block, window_at].astype(jnp.float32)
        chosen = jnp.where(source_part == 0, rows[:sources], rows[sources:])
        for row in range(8):
            turned[:, row, :] = pltpu.roll(chosen, (NS - row) % NS, 1)
        for source in range(sources):
            base = turned[source]
            for first in range(0, LAG_ROWS, 16):
                pair = [pltpu.roll(base, (LAGS // 2 - first - 8 * at) % NS, 1) for at in range(2)]
                lagged[source, first : first + 16, :] = jnp.concatenate(pair, axis=0).astype(jnp.bfloat16)
        term = lax.dot_general(
            lagged[...].reshape(sources * LAG_ROWS, NS),
            gathered[:, window_at].reshape(blocks * channels, NS),
            (((1,), (1,)), ((), ())),
            preferred_element_type=jnp.float32,
        )
        total = term if total is None else total + term
    return total


def corr_pair_kernel(scale, place, gathered, own, other, turned, lagged):
    total = lag_sums(place, gathered, turned, lagged) * scale
    half = total.shape[1] // 2
    first, second = total[:, :half], total[:, half:]
    is_first = place[0] == 0
    kept = jnp.where(is_first, first, second)
    sent = jnp.where(is_first, second, first).astype(jnp.bfloat16)
    for source in range(own.shape[0]):
        at = source * LAG_ROWS
        own[source] = kept[at : at + LAGS]
        other[source] = sent[at : at + LAG_ROWS]


def corr_all_kernel(scale, place, gathered, own, turned, lagged):
    total = lag_sums(place, gathered, turned, lagged) * scale
    for source in range(own.shape[0]):
        own[source] = total[source * LAG_ROWS : source * LAG_ROWS + LAGS]


def whole_in_vmem(count):
    return [pl.BlockSpec(memory_space=pltpu.VMEM)] * count


def local(tables, strain_raw, fir_taps, live_mask, window_start):
    channels = strain_raw.shape[0]
    windows = window_start.shape[0]
    groups = lax.axis_size("win")
    blocks = lax.axis_size("chan")
    win_at = lax.axis_index("win")
    chan_at = lax.axis_index("chan")
    record = lax.all_gather(strain_raw, "win", axis=1, tiled=True)
    padded = jnp.concatenate([fir_taps, jnp.zeros((REACH + DECIM - TAPS,), fir_taps.dtype)])
    band = jnp.tile(padded, BLOCK)[: BLOCK * REACH].reshape(BLOCK, REACH).T
    params = pltpu.CompilerParams(vmem_limit_bytes=VMEM_LIMIT)
    smem = pl.BlockSpec(memory_space=pltpu.SMEM)
    series = pl.pallas_call(
        lambda *refs: whiten_kernel(windows, *refs),
        out_shape=jax.ShapeDtypeStruct((windows, channels, NS), jnp.bfloat16),
        in_specs=[smem] + whole_in_vmem(9),
        out_specs=pl.BlockSpec(memory_space=pltpu.VMEM),
        compiler_params=params,
        name="whiten",
    )(window_start, record, band, *tables, live_mask.astype(jnp.float32)[:, None])
    gathered = lax.all_gather(series, "chan", axis=0, tiled=False)
    place = jnp.stack([win_at, chan_at]).astype(jnp.int32)
    scale = 1.0 / (math.sqrt(NS) * math.sqrt(windows * groups))
    sources = channels // STRIDE
    scratch = [
        pltpu.VMEM((sources, 8, NS), jnp.float32),
        pltpu.VMEM((sources, LAG_ROWS, NS), jnp.bfloat16),
    ]
    total = blocks * channels
    if groups == 2:
        own, other = pl.pallas_call(
            lambda *refs: corr_pair_kernel(scale, *refs),
            out_shape=[
                jax.ShapeDtypeStruct((sources, LAGS, total // 2), jnp.float32),
                jax.ShapeDtypeStruct((sources, LAG_ROWS, total // 2), jnp.bfloat16),
            ],
            in_specs=[smem] + whole_in_vmem(1),
            out_specs=whole_in_vmem(2),
            scratch_shapes=scratch,
            compiler_params=params,
            name="correlate",
        )(place, gathered)
        arrived = lax.ppermute(other, "win", [(0, 1), (1, 0)])
        return own + arrived[:, :LAGS].astype(jnp.float32)
    own = pl.pallas_call(
        lambda *refs: corr_all_kernel(scale, *refs),
        out_shape=jax.ShapeDtypeStruct((sources, LAGS, total), jnp.float32),
        in_specs=[smem] + whole_in_vmem(1),
        out_specs=pl.BlockSpec(memory_space=pltpu.VMEM),
        scratch_shapes=scratch,
        compiler_params=params,
        name="correlate",
    )(place, gathered)
    return lax.psum_scatter(own, "win", scatter_dimension=2, tiled=True)


def solution(mesh):
    in_specs = (P("chan", "win"), P(), P("chan"), P("win"))
    out_specs = P("chan", None, "win")

    def run(strain_raw, fir_taps, live_mask, window_start):
        tables = [jnp.asarray(table) for table in build_tables()]
        mapped = jax.shard_map(
            lambda tables, *args: local(tables, *args),
            mesh=mesh,
            in_specs=(P(),) + in_specs,
            out_specs=out_specs,
            check_vma=False,
        )
        return mapped(tables, strain_raw, fir_taps, live_mask, window_start)

    return run
```

```python
import math

import jax
import jax.numpy as jnp
import ml_dtypes
import numpy as np
from jax import lax
from jax.experimental import pallas as pl
from jax.experimental.pallas import tpu as pltpu
from jax.sharding import PartitionSpec as P

NS = 1024
DECIM = 4
TAPS = 128
HALF = 32
LAGS = 101
STRIDE = 2
EPSILON = 1e-06

FOLD = NS // 2
BLOCK = 128
REACH = BLOCK * DECIM + TAPS
LAG_ROWS = 112
VMEM_LIMIT = 48 * 1024 * 1024


def split_table(table):
    high = table.astype(ml_dtypes.bfloat16)
    low = (table - high.astype(np.float64)).astype(ml_dtypes.bfloat16)
    return high, low


def build_tables():
    time_at = np.arange(FOLD)
    forward = []
    inverse = []
    for parity in range(2):
        bins = 2 * np.arange(NS // 4) + parity
        angle = 2.0 * np.pi * ((time_at[:, None] * bins[None, :]) % NS) / NS
        cosine = np.cos(angle)
        sine = -np.sin(angle)
        weight = np.full((2 * bins.size,), 2.0 / math.sqrt(NS))
        if parity == 0:
            sine[:, 0] = np.cos(np.pi * time_at)
            weight[0] = 1.0 / math.sqrt(NS)
            weight[bins.size] = 1.0 / math.sqrt(NS)
        table = np.concatenate([cosine, sine], axis=1)
        forward.append(table)
        inverse.append((table * weight[None, :]).T)
    order = np.concatenate([np.arange(0, FOLD, 2), np.arange(1, FOLD, 2), [FOLD]])
    place = np.zeros((FOLD + 1,), np.int64)
    place[order] = np.arange(FOLD + 1)
    counts = np.zeros((FOLD + 1, FOLD + 1))
    for column, bin_at in enumerate(order):
        for offset in range(-HALF, HALF + 1):
            seen = (bin_at + offset) % NS
            counts[place[min(seen, NS - seen)], column] += 1.0
    mean_table = counts[:FOLD, :FOLD].astype(ml_dtypes.bfloat16)
    edge = np.zeros((8, FOLD), np.float32)
    edge[0] = counts[FOLD, :FOLD]
    edge[1] = counts[:FOLD, FOLD]
    forward_high, forward_low = split_table(np.stack(forward))
    inverse_high, inverse_low = split_table(np.stack(inverse))
    return forward_high, forward_low, inverse_high, inverse_low, mean_table, edge


def dot(left, right):
    return jnp.dot(left, right, preferred_element_type=jnp.float32)


def split_dot(value, high, low):
    rows = value.shape[0]
    value_high = value.astype(jnp.bfloat16)
    value_low = (value - value_high.astype(jnp.float32)).astype(jnp.bfloat16)
    both = dot(jnp.concatenate([value_high, value_low], axis=0), high)
    return both[:rows] + both[rows:] + dot(value_high, low)


def whiten_kernel(windows, starts, record, band, forward_high, forward_low, inverse_high, inverse_low,
                  mean_table, edge, live, out):
    channels, length = record.shape
    wide = record[...].astype(jnp.float32)
    pieces = []
    for window_at in range(windows):
        start = starts[window_at]
        rolled = pltpu.roll(wide, lax.rem(length - start, length), 1).astype(jnp.bfloat16)
        parts = [
            dot(rolled[:, at * BLOCK * DECIM : at * BLOCK * DECIM + REACH], band[...])
            for at in range(NS // BLOCK)
        ]
        pieces.append(jnp.concatenate(parts, axis=1))
    decimated = jnp.concatenate(pieces, axis=0)
    first, second = decimated[:, :FOLD], decimated[:, FOLD:]
    even = split_dot(first + second, forward_high[0], forward_low[0])
    odd = split_dot(first - second, forward_high[1], forward_low[1])
    quarter = NS // 4
    real_part = jnp.concatenate([even[:, :quarter], odd[:, :quarter]], axis=1)
    imag_part = jnp.concatenate([even[:, quarter:], odd[:, quarter:]], axis=1)
    at_zero = lax.broadcasted_iota(jnp.int32, real_part.shape, 1) == 0
    amplitude = jnp.sqrt(real_part * real_part + jnp.where(at_zero, 0.0, imag_part * imag_part))
    top = jnp.abs(imag_part[:, 0:1])
    amp_high = amplitude.astype(jnp.bfloat16)
    amp_low = (amplitude - amp_high.astype(jnp.float32)).astype(jnp.bfloat16)
    summed = dot(amp_high, mean_table[...]) + dot(amp_low, mean_table[...]) + top * edge[0:1, :]
    summed_top = jnp.sum(amplitude * edge[1:2, :], axis=1, keepdims=True) + top
    width = 2 * HALF + 1
    scale = 1.0 / (summed * (1.0 / width) + EPSILON)
    scale_top = 1.0 / (summed_top * (1.0 / width) + EPSILON)
    white_real = real_part * scale
    white_imag = imag_part * jnp.where(at_zero, scale_top, scale)
    white_even = jnp.concatenate([white_real[:, :quarter], white_imag[:, :quarter]], axis=1)
    white_odd = jnp.concatenate([white_real[:, quarter:], white_imag[:, quarter:]], axis=1)
    from_even = split_dot(white_even, inverse_high[0], inverse_low[0])
    from_odd = split_dot(white_odd, inverse_high[1], inverse_low[1])
    series = jnp.concatenate([from_even + from_odd, from_even - from_odd], axis=1)
    for window_at in range(windows):
        rows = series[window_at * channels : (window_at + 1) * channels]
        out[window_at] = (rows * live[...]).astype(jnp.bfloat16)


def lag_sums(place, gathered, turned, lagged):
    blocks, windows, channels, _ = gathered.shape
    sources = channels // STRIDE
    chan_at = place[1]
    source_block = chan_at // STRIDE * STRIDE
    source_part = lax.rem(chan_at, STRIDE)
    total = None
    for window_at in range(windows):
        rows = gathered[source_block, window_at].astype(jnp.float32)
        chosen = jnp.where(source_part == 0, rows[:sources], rows[sources:])
        for row in range(8):
            turned[:, row, :] = pltpu.roll(chosen, (NS - row) % NS, 1)
        for source in range(sources):
            base = turned[source]
            for first in range(0, LAG_ROWS, 16):
                pair = [pltpu.roll(base, (LAGS // 2 - first - 8 * at) % NS, 1) for at in range(2)]
                lagged[source, first : first + 16, :] = jnp.concatenate(pair, axis=0).astype(jnp.bfloat16)
        term = lax.dot_general(
            lagged[...].reshape(sources * LAG_ROWS, NS),
            gathered[:, window_at].reshape(blocks * channels, NS),
            (((1,), (1,)), ((), ())),
            preferred_element_type=jnp.float32,
        )
        total = term if total is None else total + term
    return total


def gather_corr_kernel(scale, series, out, held, turned, lagged, outgoing, arrived,
                       sent, landed, swap_sent, swap_landed):
    blocks, windows, channels, _ = held.shape
    sources = channels // STRIDE
    layers = blocks // 4
    win_at = lax.axis_index("win")
    me = lax.axis_index("chan")
    layer, core = me // 4, lax.rem(me, 2)
    lane = lax.rem(me, 4)
    beside = layer * 4 + lax.rem(lane + 2, 4)
    twin = me + 1 - 2 * core
    twin_lane = lane + 1 - 2 * core
    other_lane = lax.rem(lane + 2, 4)
    partner = 1 - win_at
    above, below = me + 4, me - 4
    has_above, has_below = layer < layers - 1, layer > 0
    mesh_id = pl.DeviceIdType.MESH

    barrier = pltpu.get_barrier_semaphore()
    pl.semaphore_signal(barrier, inc=1, device_id=(win_at, beside), device_id_type=mesh_id)
    pl.semaphore_signal(barrier, inc=1, device_id=(win_at, twin), device_id_type=mesh_id)
    pl.semaphore_signal(barrier, inc=1, device_id=(partner, me), device_id_type=mesh_id)

    @pl.when(has_above)
    def _():
        pl.semaphore_signal(barrier, inc=1, device_id=(win_at, above), device_id_type=mesh_id)

    @pl.when(has_below)
    def _():
        pl.semaphore_signal(barrier, inc=1, device_id=(win_at, below), device_id_type=mesh_id)

    held[me] = series[...]
    pl.semaphore_wait(barrier, 3 + has_above.astype(jnp.int32) + has_below.astype(jnp.int32))

    def move(way, block, target):
        return pltpu.make_async_remote_copy(
            src_ref=held.at[block],
            dst_ref=held.at[block],
            send_sem=sent.at[way, block],
            recv_sem=landed.at[block],
            device_id=(win_at, target),
            device_id_type=mesh_id,
        )

    def up(block):
        return move(0, block, above)

    def down(block):
        return move(1, block, below)

    def across(block):
        return move(2, block, beside)

    def over(block):
        return move(3, block, twin)

    def await_block(block):
        move(2, block, beside).wait_recv()

    def when(condition, action):
        @pl.when(condition)
        def _():
            action()

    when(has_above, lambda: up(me).start())
    when(has_below, lambda: down(me).start())
    across(me).start()
    over(me).start()

    await_block(twin)
    source_block = me // STRIDE * STRIDE
    source_part = lax.rem(me, STRIDE)

    def build(window_at, carry):
        rows = held[source_block, window_at].astype(jnp.float32)
        chosen = jnp.where(source_part == 0, rows[:sources], rows[sources:])
        for row in range(8):
            turned[:, row, :] = pltpu.roll(chosen, (NS - row) % NS, 1)

        def build_source(source, carry):
            base = turned[source]
            for first in range(0, LAG_ROWS, 16):
                pair = [pltpu.roll(base, (LAGS // 2 - first - 8 * at) % NS, 1) for at in range(2)]
                lagged[window_at, source, first : first + 16, :] = jnp.concatenate(pair, axis=0).astype(jnp.bfloat16)
            return carry

        return lax.fori_loop(0, sources, build_source, carry)

    def pass_lane(distance):
        for sign in (-1, 1):
            origin = layer + sign * distance
            block = me + 4 * sign * distance
            exists = (origin >= 0) if sign < 0 else (origin < layers)
            further = has_above if sign < 0 else has_below

            def relay():
                await_block(block)
                when(further, lambda: (up if sign < 0 else down)(block).start())
                across(block).start()
                over(block).start()

            when(exists, relay)

    def pass_beside(distance):
        for sign in (-1, 1) if distance else (1,):
            origin = layer + sign * distance
            block = origin * 4 + other_lane
            exists = (origin >= 0) if sign < 0 else (origin < layers)

            def relay():
                await_block(block)
                over(block).start()

            when(exists, relay)

    lax.fori_loop(0, windows, build, 0)
    pass_lane(1)
    pass_beside(0)
    for distance in range(2, layers):
        pass_lane(distance)
        pass_beside(distance - 1)
    pass_beside(layers - 1)
    for at in range(layers):
        across_twin = at * 4 + lax.rem(twin_lane + 2, 4)
        await_block(across_twin)
        mine = at * 4 + twin_lane
        when(mine != twin, lambda: await_block(mine))

    half_blocks = blocks // 2

    def half_sums(half):
        total = None
        for window_at in range(windows):
            term = lax.dot_general(
                lagged[window_at].reshape(sources * LAG_ROWS, NS),
                held[pl.ds(half * half_blocks, half_blocks), window_at].reshape(half_blocks * channels, NS),
                (((1,), (1,)), ((), ())),
                preferred_element_type=jnp.float32,
            )
            total = term if total is None else total + term
        return total * scale

    outgoing[...] = half_sums(partner).astype(jnp.bfloat16).reshape(outgoing.shape)
    swap = pltpu.make_async_remote_copy(
        src_ref=outgoing,
        dst_ref=arrived,
        send_sem=swap_sent,
        recv_sem=swap_landed,
        device_id=(partner, me),
        device_id_type=mesh_id,
    )
    swap.start()
    kept = half_sums(win_at).reshape(outgoing.shape)
    swap.wait()
    total = kept + arrived[...].astype(jnp.float32)
    for source in range(sources):
        out[source] = total[source, :LAGS]

    for at in range(layers):
        block = at * 4 + lane
        when(jnp.logical_and(has_above, at <= layer), lambda: up(block).wait_send())
        when(jnp.logical_and(has_below, at >= layer), lambda: down(block).wait_send())
        across(block).wait_send()
        over(block).wait_send()
        over(at * 4 + other_lane).wait_send()


def corr_all_kernel(scale, place, gathered, own, turned, lagged):
    total = lag_sums(place, gathered, turned, lagged) * scale
    for source in range(own.shape[0]):
        own[source] = total[source * LAG_ROWS : source * LAG_ROWS + LAGS]


def whole_in_vmem(count):
    return [pl.BlockSpec(memory_space=pltpu.VMEM)] * count


def local(tables, strain_raw, fir_taps, live_mask, window_start):
    channels = strain_raw.shape[0]
    windows = window_start.shape[0]
    groups = lax.axis_size("win")
    blocks = lax.axis_size("chan")
    win_at = lax.axis_index("win")
    chan_at = lax.axis_index("chan")
    record = lax.all_gather(strain_raw, "win", axis=1, tiled=True)
    padded = jnp.concatenate([fir_taps, jnp.zeros((REACH + DECIM - TAPS,), fir_taps.dtype)])
    band = jnp.tile(padded, BLOCK)[: BLOCK * REACH].reshape(BLOCK, REACH).T
    params = pltpu.CompilerParams(vmem_limit_bytes=VMEM_LIMIT)
    smem = pl.BlockSpec(memory_space=pltpu.SMEM)
    series = pl.pallas_call(
        lambda *refs: whiten_kernel(windows, *refs),
        out_shape=jax.ShapeDtypeStruct((windows, channels, NS), jnp.bfloat16),
        in_specs=[smem] + whole_in_vmem(9),
        out_specs=pl.BlockSpec(memory_space=pltpu.VMEM),
        compiler_params=params,
        name="whiten",
    )(window_start, record, band, *tables, live_mask.astype(jnp.float32)[:, None])
    scale = 1.0 / (math.sqrt(NS) * math.sqrt(windows * groups))
    sources = channels // STRIDE
    total = blocks * channels
    if groups == 2 and blocks == 16:
        return pl.pallas_call(
            lambda *refs: gather_corr_kernel(scale, *refs),
            out_shape=jax.ShapeDtypeStruct((sources, LAGS, total // 2), jnp.float32),
            in_specs=whole_in_vmem(1),
            out_specs=pl.BlockSpec(memory_space=pltpu.VMEM),
            scratch_shapes=[
                pltpu.VMEM((blocks, windows, channels, NS), jnp.bfloat16),
                pltpu.VMEM((sources, 8, NS), jnp.float32),
                pltpu.VMEM((windows, sources, LAG_ROWS, NS), jnp.bfloat16),
                pltpu.VMEM((sources, LAG_ROWS, total // 2), jnp.bfloat16),
                pltpu.VMEM((sources, LAG_ROWS, total // 2), jnp.bfloat16),
                pltpu.SemaphoreType.DMA((4, blocks)),
                pltpu.SemaphoreType.DMA((blocks,)),
                pltpu.SemaphoreType.DMA,
                pltpu.SemaphoreType.DMA,
            ],
            compiler_params=pltpu.CompilerParams(
                vmem_limit_bytes=VMEM_LIMIT, collective_id=0, has_side_effects=True
            ),
            name="gather_correlate",
        )(series)
    gathered = lax.all_gather(series, "chan", axis=0, tiled=False)
    place = jnp.stack([win_at, chan_at]).astype(jnp.int32)
    scratch = [
        pltpu.VMEM((sources, 8, NS), jnp.float32),
        pltpu.VMEM((sources, LAG_ROWS, NS), jnp.bfloat16),
    ]
    own = pl.pallas_call(
        lambda *refs: corr_all_kernel(scale, *refs),
        out_shape=jax.ShapeDtypeStruct((sources, LAGS, total), jnp.float32),
        in_specs=[smem] + whole_in_vmem(1),
        out_specs=pl.BlockSpec(memory_space=pltpu.VMEM),
        scratch_shapes=scratch,
        compiler_params=params,
        name="correlate",
    )(place, gathered)
    return lax.psum_scatter(own, "win", scatter_dimension=2, tiled=True)


def solution(mesh):
    in_specs = (P("chan", "win"), P(), P("chan"), P("win"))
    out_specs = P("chan", None, "win")

    def run(strain_raw, fir_taps, live_mask, window_start):
        tables = [jnp.asarray(table) for table in build_tables()]
        mapped = jax.shard_map(
            lambda tables, *args: local(tables, *args),
            mesh=mesh,
            in_specs=(P(),) + in_specs,
            out_specs=out_specs,
            check_vma=False,
        )
        return mapped(tables, strain_raw, fir_taps, live_mask, window_start)

    return run
```

```python
import math

import jax
import jax.numpy as jnp
import ml_dtypes
import numpy as np
from jax import lax
from jax.experimental import pallas as pl
from jax.experimental.pallas import tpu as pltpu
from jax.sharding import PartitionSpec as P

NS = 1024
DECIM = 4
TAPS = 128
HALF = 32
LAGS = 101
STRIDE = 2
EPSILON = 1e-06

FOLD = NS // 2
BLOCK = 128
REACH = BLOCK * DECIM + TAPS
LAG_ROWS = 112
CHUNKS = 2
VMEM_LIMIT = 48 * 1024 * 1024


def split_table(table):
    high = table.astype(ml_dtypes.bfloat16)
    low = (table - high.astype(np.float64)).astype(ml_dtypes.bfloat16)
    return high, low


def build_tables():
    time_at = np.arange(FOLD)
    forward = []
    inverse = []
    for parity in range(2):
        bins = 2 * np.arange(NS // 4) + parity
        angle = 2.0 * np.pi * ((time_at[:, None] * bins[None, :]) % NS) / NS
        cosine = np.cos(angle)
        sine = -np.sin(angle)
        weight = np.full((2 * bins.size,), 2.0 / math.sqrt(NS))
        if parity == 0:
            sine[:, 0] = np.cos(np.pi * time_at)
            weight[0] = 1.0 / math.sqrt(NS)
            weight[bins.size] = 1.0 / math.sqrt(NS)
        table = np.concatenate([cosine, sine], axis=1)
        forward.append(table)
        inverse.append((table * weight[None, :]).T)
    order = np.concatenate([np.arange(0, FOLD, 2), np.arange(1, FOLD, 2), [FOLD]])
    place = np.zeros((FOLD + 1,), np.int64)
    place[order] = np.arange(FOLD + 1)
    counts = np.zeros((FOLD + 1, FOLD + 1))
    for column, bin_at in enumerate(order):
        for offset in range(-HALF, HALF + 1):
            seen = (bin_at + offset) % NS
            counts[place[min(seen, NS - seen)], column] += 1.0
    mean_table = counts[:FOLD, :FOLD].astype(ml_dtypes.bfloat16)
    edge = np.zeros((8, FOLD), np.float32)
    edge[0] = counts[FOLD, :FOLD]
    edge[1] = counts[:FOLD, FOLD]
    forward_high, forward_low = split_table(np.stack(forward))
    inverse_high, inverse_low = split_table(np.stack(inverse))
    return forward_high, forward_low, inverse_high, inverse_low, mean_table, edge


def dot(left, right):
    return jnp.dot(left, right, preferred_element_type=jnp.float32)


def split_dot(value, high, low):
    rows = value.shape[0]
    value_high = value.astype(jnp.bfloat16)
    value_low = (value - value_high.astype(jnp.float32)).astype(jnp.bfloat16)
    both = dot(jnp.concatenate([value_high, value_low], axis=0), high)
    return both[:rows] + both[rows:] + dot(value_high, low)


def whiten_kernel(windows, starts, record, band, forward_high, forward_low, inverse_high, inverse_low,
                  mean_table, edge, live, out):
    channels, length = record.shape
    wide = record[...].astype(jnp.float32)
    pieces = []
    for window_at in range(windows):
        start = starts[window_at]
        rolled = pltpu.roll(wide, lax.rem(length - start, length), 1).astype(jnp.bfloat16)
        parts = [
            dot(rolled[:, at * BLOCK * DECIM : at * BLOCK * DECIM + REACH], band[...])
            for at in range(NS // BLOCK)
        ]
        pieces.append(jnp.concatenate(parts, axis=1))
    decimated = jnp.concatenate(pieces, axis=0)
    first, second = decimated[:, :FOLD], decimated[:, FOLD:]
    even = split_dot(first + second, forward_high[0], forward_low[0])
    odd = split_dot(first - second, forward_high[1], forward_low[1])
    quarter = NS // 4
    real_part = jnp.concatenate([even[:, :quarter], odd[:, :quarter]], axis=1)
    imag_part = jnp.concatenate([even[:, quarter:], odd[:, quarter:]], axis=1)
    at_zero = lax.broadcasted_iota(jnp.int32, real_part.shape, 1) == 0
    amplitude = jnp.sqrt(real_part * real_part + jnp.where(at_zero, 0.0, imag_part * imag_part))
    top = jnp.abs(imag_part[:, 0:1])
    amp_high = amplitude.astype(jnp.bfloat16)
    amp_low = (amplitude - amp_high.astype(jnp.float32)).astype(jnp.bfloat16)
    summed = dot(amp_high, mean_table[...]) + dot(amp_low, mean_table[...]) + top * edge[0:1, :]
    summed_top = jnp.sum(amplitude * edge[1:2, :], axis=1, keepdims=True) + top
    width = 2 * HALF + 1
    scale = 1.0 / (summed * (1.0 / width) + EPSILON)
    scale_top = 1.0 / (summed_top * (1.0 / width) + EPSILON)
    white_real = real_part * scale
    white_imag = imag_part * jnp.where(at_zero, scale_top, scale)
    white_even = jnp.concatenate([white_real[:, :quarter], white_imag[:, :quarter]], axis=1)
    white_odd = jnp.concatenate([white_real[:, quarter:], white_imag[:, quarter:]], axis=1)
    from_even = split_dot(white_even, inverse_high[0], inverse_low[0])
    from_odd = split_dot(white_odd, inverse_high[1], inverse_low[1])
    series = jnp.concatenate([from_even + from_odd, from_even - from_odd], axis=1)
    for window_at in range(windows):
        rows = series[window_at * channels : (window_at + 1) * channels]
        out[window_at] = (rows * live[...]).astype(jnp.bfloat16)


def lag_sums(place, gathered, turned, lagged):
    blocks, windows, channels, _ = gathered.shape
    sources = channels // STRIDE
    chan_at = place[1]
    source_block = chan_at // STRIDE * STRIDE
    source_part = lax.rem(chan_at, STRIDE)
    total = None
    for window_at in range(windows):
        rows = gathered[source_block, window_at].astype(jnp.float32)
        chosen = jnp.where(source_part == 0, rows[:sources], rows[sources:])
        for row in range(8):
            turned[:, row, :] = pltpu.roll(chosen, (NS - row) % NS, 1)
        for source in range(sources):
            base = turned[source]
            for first in range(0, LAG_ROWS, 16):
                pair = [pltpu.roll(base, (LAGS // 2 - first - 8 * at) % NS, 1) for at in range(2)]
                lagged[source, first : first + 16, :] = jnp.concatenate(pair, axis=0).astype(jnp.bfloat16)
        term = lax.dot_general(
            lagged[...].reshape(sources * LAG_ROWS, NS),
            gathered[:, window_at].reshape(blocks * channels, NS),
            (((1,), (1,)), ((), ())),
            preferred_element_type=jnp.float32,
        )
        total = term if total is None else total + term
    return total


def gather_corr_kernel(scale, series, out, held, turned, lagged, outgoing, arrived,
                       sent, landed, swap_sent, swap_landed):
    blocks, windows, channels, _ = held.shape
    sources = channels // STRIDE
    layers = blocks // 4
    win_at = lax.axis_index("win")
    me = lax.axis_index("chan")
    layer, core = me // 4, lax.rem(me, 2)
    lane = lax.rem(me, 4)
    beside = layer * 4 + lax.rem(lane + 2, 4)
    twin = me + 1 - 2 * core
    twin_lane = lane + 1 - 2 * core
    other_lane = lax.rem(lane + 2, 4)
    partner = 1 - win_at
    above, below = me + 4, me - 4
    has_above, has_below = layer < layers - 1, layer > 0
    mesh_id = pl.DeviceIdType.MESH

    barrier = pltpu.get_barrier_semaphore()
    pl.semaphore_signal(barrier, inc=1, device_id=(win_at, beside), device_id_type=mesh_id)
    pl.semaphore_signal(barrier, inc=1, device_id=(win_at, twin), device_id_type=mesh_id)
    pl.semaphore_signal(barrier, inc=1, device_id=(partner, me), device_id_type=mesh_id)

    @pl.when(has_above)
    def _():
        pl.semaphore_signal(barrier, inc=1, device_id=(win_at, above), device_id_type=mesh_id)

    @pl.when(has_below)
    def _():
        pl.semaphore_signal(barrier, inc=1, device_id=(win_at, below), device_id_type=mesh_id)

    held[me] = series[...]
    pl.semaphore_wait(barrier, 3 + has_above.astype(jnp.int32) + has_below.astype(jnp.int32))

    chunk = windows // CHUNKS

    def move(way, block, part, target):
        span = held.at[block, pl.ds(part * chunk, chunk)]
        return pltpu.make_async_remote_copy(
            src_ref=span,
            dst_ref=span,
            send_sem=sent.at[way, block, part],
            recv_sem=landed.at[block, part],
            device_id=(win_at, target),
            device_id_type=mesh_id,
        )

    def up(block, part):
        return move(0, block, part, above)

    def down(block, part):
        return move(1, block, part, below)

    def across(block, part):
        return move(2, block, part, beside)

    def over(block, part):
        return move(3, block, part, twin)

    def await_block(block, part):
        across(block, part).wait_recv()

    def when(condition, action):
        @pl.when(condition)
        def _():
            action()

    for part in range(CHUNKS):
        when(has_above, lambda: up(me, part).start())
        when(has_below, lambda: down(me, part).start())
        across(me, part).start()
        over(me, part).start()

    source_block = me // STRIDE * STRIDE
    source_part = lax.rem(me, STRIDE)

    def build(window_at):
        rows = held[source_block, window_at].astype(jnp.float32)
        chosen = jnp.where(source_part == 0, rows[:sources], rows[sources:])
        for row in range(8):
            turned[:, row, :] = pltpu.roll(chosen, (NS - row) % NS, 1)

        def build_source(source, carry):
            base = turned[source]
            for first in range(0, LAG_ROWS, 16):
                pair = [pltpu.roll(base, (LAGS // 2 - first - 8 * at) % NS, 1) for at in range(2)]
                lagged[window_at, source, first : first + 16, :] = jnp.concatenate(pair, axis=0).astype(jnp.bfloat16)
            return carry

        lax.fori_loop(0, sources, build_source, 0)

    def pass_lane(distance, part):
        for sign in (-1, 1):
            origin = layer + sign * distance
            block = me + 4 * sign * distance
            exists = (origin >= 0) if sign < 0 else (origin < layers)
            further = has_above if sign < 0 else has_below

            def relay():
                await_block(block, part)
                when(further, lambda: (up if sign < 0 else down)(block, part).start())
                across(block, part).start()
                over(block, part).start()

            when(exists, relay)

    def pass_beside(distance, part):
        for sign in (-1, 1) if distance else (1,):
            origin = layer + sign * distance
            block = origin * 4 + other_lane
            exists = (origin >= 0) if sign < 0 else (origin < layers)

            def relay():
                await_block(block, part)
                over(block, part).start()

            when(exists, relay)

    to_build = list(range(windows))
    for part in range(CHUNKS):
        await_block(twin, part)
    build(to_build.pop(0))
    for distance in range(1, layers):
        for part in range(CHUNKS):
            pass_lane(distance, part)
            if to_build:
                build(to_build.pop(0))
            pass_beside(distance - 1, part)
    while to_build:
        build(to_build.pop(0))
    half_blocks = blocks // 2

    def window_sums(half, window_at):
        return lax.dot_general(
            lagged[window_at].reshape(sources * LAG_ROWS, NS),
            held[pl.ds(half * half_blocks, half_blocks), window_at].reshape(half_blocks * channels, NS),
            (((1,), (1,)), ((), ())),
            preferred_element_type=jnp.float32,
        )

    for part in range(CHUNKS):
        pass_beside(layers - 1, part)
    partial = None
    for part in range(CHUNKS):
        for at in range(layers):
            await_block(at * 4 + lax.rem(twin_lane + 2, 4), part)
            mine = at * 4 + twin_lane
            when(mine != twin, lambda: await_block(mine, part))
        for window_at in range(part * chunk, (part + 1) * chunk):
            term = window_sums(partner, window_at)
            partial = term if partial is None else partial + term

    def own_sums():
        total = None
        for window_at in range(windows):
            term = window_sums(win_at, window_at)
            total = term if total is None else total + term
        return total * scale

    outgoing[...] = (partial * scale).astype(jnp.bfloat16).reshape(outgoing.shape)
    swap = pltpu.make_async_remote_copy(
        src_ref=outgoing,
        dst_ref=arrived,
        send_sem=swap_sent,
        recv_sem=swap_landed,
        device_id=(partner, me),
        device_id_type=mesh_id,
    )
    swap.start()
    kept = own_sums().reshape(outgoing.shape)
    swap.wait()
    total = kept + arrived[...].astype(jnp.float32)
    for source in range(sources):
        out[source] = total[source, :LAGS]

    for at in range(layers):
        block = at * 4 + lane
        for part in range(CHUNKS):
            when(jnp.logical_and(has_above, at <= layer), lambda: up(block, part).wait_send())
            when(jnp.logical_and(has_below, at >= layer), lambda: down(block, part).wait_send())
            across(block, part).wait_send()
            over(block, part).wait_send()
            over(at * 4 + other_lane, part).wait_send()


def corr_all_kernel(scale, place, gathered, own, turned, lagged):
    total = lag_sums(place, gathered, turned, lagged) * scale
    for source in range(own.shape[0]):
        own[source] = total[source * LAG_ROWS : source * LAG_ROWS + LAGS]


def whole_in_vmem(count):
    return [pl.BlockSpec(memory_space=pltpu.VMEM)] * count


def local(tables, strain_raw, fir_taps, live_mask, window_start):
    channels = strain_raw.shape[0]
    windows = window_start.shape[0]
    groups = lax.axis_size("win")
    blocks = lax.axis_size("chan")
    win_at = lax.axis_index("win")
    chan_at = lax.axis_index("chan")
    record = lax.all_gather(strain_raw, "win", axis=1, tiled=True)
    padded = jnp.concatenate([fir_taps, jnp.zeros((REACH + DECIM - TAPS,), fir_taps.dtype)])
    band = jnp.tile(padded, BLOCK)[: BLOCK * REACH].reshape(BLOCK, REACH).T
    params = pltpu.CompilerParams(vmem_limit_bytes=VMEM_LIMIT)
    smem = pl.BlockSpec(memory_space=pltpu.SMEM)
    series = pl.pallas_call(
        lambda *refs: whiten_kernel(windows, *refs),
        out_shape=jax.ShapeDtypeStruct((windows, channels, NS), jnp.bfloat16),
        in_specs=[smem] + whole_in_vmem(9),
        out_specs=pl.BlockSpec(memory_space=pltpu.VMEM),
        compiler_params=params,
        name="whiten",
    )(window_start, record, band, *tables, live_mask.astype(jnp.float32)[:, None])
    scale = 1.0 / (math.sqrt(NS) * math.sqrt(windows * groups))
    sources = channels // STRIDE
    total = blocks * channels
    if groups == 2 and blocks == 16:
        return pl.pallas_call(
            lambda *refs: gather_corr_kernel(scale, *refs),
            out_shape=jax.ShapeDtypeStruct((sources, LAGS, total // 2), jnp.float32),
            in_specs=whole_in_vmem(1),
            out_specs=pl.BlockSpec(memory_space=pltpu.VMEM),
            scratch_shapes=[
                pltpu.VMEM((blocks, windows, channels, NS), jnp.bfloat16),
                pltpu.VMEM((sources, 8, NS), jnp.float32),
                pltpu.VMEM((windows, sources, LAG_ROWS, NS), jnp.bfloat16),
                pltpu.VMEM((sources, LAG_ROWS, total // 2), jnp.bfloat16),
                pltpu.VMEM((sources, LAG_ROWS, total // 2), jnp.bfloat16),
                pltpu.SemaphoreType.DMA((4, blocks, CHUNKS)),
                pltpu.SemaphoreType.DMA((blocks, CHUNKS)),
                pltpu.SemaphoreType.DMA,
                pltpu.SemaphoreType.DMA,
            ],
            compiler_params=pltpu.CompilerParams(
                vmem_limit_bytes=VMEM_LIMIT, collective_id=0, has_side_effects=True
            ),
            name="gather_correlate",
        )(series)
    gathered = lax.all_gather(series, "chan", axis=0, tiled=False)
    place = jnp.stack([win_at, chan_at]).astype(jnp.int32)
    scratch = [
        pltpu.VMEM((sources, 8, NS), jnp.float32),
        pltpu.VMEM((sources, LAG_ROWS, NS), jnp.bfloat16),
    ]
    own = pl.pallas_call(
        lambda *refs: corr_all_kernel(scale, *refs),
        out_shape=jax.ShapeDtypeStruct((sources, LAGS, total), jnp.float32),
        in_specs=[smem] + whole_in_vmem(1),
        out_specs=pl.BlockSpec(memory_space=pltpu.VMEM),
        scratch_shapes=scratch,
        compiler_params=params,
        name="correlate",
    )(place, gathered)
    return lax.psum_scatter(own, "win", scatter_dimension=2, tiled=True)


def solution(mesh):
    in_specs = (P("chan", "win"), P(), P("chan"), P("win"))
    out_specs = P("chan", None, "win")

    def run(strain_raw, fir_taps, live_mask, window_start):
        tables = [jnp.asarray(table) for table in build_tables()]
        mapped = jax.shard_map(
            lambda tables, *args: local(tables, *args),
            mesh=mesh,
            in_specs=(P(),) + in_specs,
            out_specs=out_specs,
            check_vma=False,
        )
        return mapped(tables, strain_raw, fir_taps, live_mask, window_start)

    return run
```

```python
import math

import jax
import jax.numpy as jnp
import ml_dtypes
import numpy as np
from jax import lax
from jax.experimental import pallas as pl
from jax.experimental.pallas import tpu as pltpu
from jax.sharding import PartitionSpec as P

NS = 1024
DECIM = 4
TAPS = 128
HALF = 32
LAGS = 101
STRIDE = 2
EPSILON = 1e-06

FOLD = NS // 2
BLOCK = 128
REACH = BLOCK * DECIM + TAPS
LAG_ROWS = 112
CHUNKS = 2
VMEM_LIMIT = 60 * 1024 * 1024


def split_table(table):
    high = table.astype(ml_dtypes.bfloat16)
    low = (table - high.astype(np.float64)).astype(ml_dtypes.bfloat16)
    return high, low


def build_tables():
    time_at = np.arange(FOLD)
    forward = []
    inverse = []
    for parity in range(2):
        bins = 2 * np.arange(NS // 4) + parity
        angle = 2.0 * np.pi * ((time_at[:, None] * bins[None, :]) % NS) / NS
        cosine = np.cos(angle)
        sine = -np.sin(angle)
        weight = np.full((2 * bins.size,), 2.0 / math.sqrt(NS))
        if parity == 0:
            sine[:, 0] = np.cos(np.pi * time_at)
            weight[0] = 1.0 / math.sqrt(NS)
            weight[bins.size] = 1.0 / math.sqrt(NS)
        table = np.concatenate([cosine, sine], axis=1)
        forward.append(table)
        inverse.append((table * weight[None, :]).T)
    order = np.concatenate([np.arange(0, FOLD, 2), np.arange(1, FOLD, 2), [FOLD]])
    place = np.zeros((FOLD + 1,), np.int64)
    place[order] = np.arange(FOLD + 1)
    counts = np.zeros((FOLD + 1, FOLD + 1))
    for column, bin_at in enumerate(order):
        for offset in range(-HALF, HALF + 1):
            seen = (bin_at + offset) % NS
            counts[place[min(seen, NS - seen)], column] += 1.0
    mean_table = counts[:FOLD, :FOLD].astype(ml_dtypes.bfloat16)
    edge = np.zeros((8, FOLD), np.float32)
    edge[0] = counts[FOLD, :FOLD]
    edge[1] = counts[:FOLD, FOLD]
    forward_high, forward_low = split_table(np.stack(forward))
    inverse_high, inverse_low = split_table(np.stack(inverse))
    return forward_high, forward_low, inverse_high, inverse_low, mean_table, edge


def dot(left, right):
    return jnp.dot(left, right, preferred_element_type=jnp.float32)


def split_dot(value, high, low):
    rows = value.shape[0]
    value_high = value.astype(jnp.bfloat16)
    value_low = (value - value_high.astype(jnp.float32)).astype(jnp.bfloat16)
    both = dot(jnp.concatenate([value_high, value_low], axis=0), high)
    return both[:rows] + both[rows:] + dot(value_high, low)


def start_tables(sources, places, arrivals):
    copies = [pltpu.make_async_copy(source, place, arrivals.at[at])
              for at, (source, place) in enumerate(zip(sources, places))]
    for copy in copies:
        copy.start()
    return copies


def band_rows(taps):
    rows = jnp.concatenate([taps, jnp.zeros((1, REACH - TAPS), jnp.float32)], axis=1)
    rows = jnp.broadcast_to(rows, (BLOCK, REACH))
    row_at = lax.broadcasted_iota(jnp.int32, (BLOCK, REACH), 0)
    step = 1
    while step < BLOCK:
        rows = jnp.where(row_at // step % 2 == 1, pltpu.roll(rows, step * DECIM, 1), rows)
        step *= 2
    return rows.astype(jnp.bfloat16)


def whiten_pair_kernel(windows, starts, live, strain, taps, *refs):
    sources, out, record = refs[:6], refs[6], refs[7]
    places, (arrivals, sent, landed) = refs[8:14], refs[14:]
    copies = start_tables(sources, places, arrivals)
    win_at = lax.axis_index("win")
    partner = (1 - win_at, lax.axis_index("chan"))
    barrier = pltpu.get_barrier_semaphore()
    pl.semaphore_signal(barrier, inc=1, device_id=partner, device_id_type=pl.DeviceIdType.MESH)
    pl.semaphore_wait(barrier, 1)
    swap = pltpu.make_async_remote_copy(
        src_ref=strain,
        dst_ref=record.at[win_at],
        send_sem=sent,
        recv_sem=landed,
        device_id=partner,
        device_id_type=pl.DeviceIdType.MESH,
    )
    swap.start()
    record[win_at] = strain[...]
    band = band_rows(taps[...])
    swap.wait()
    wide = jnp.concatenate([record[0].astype(jnp.float32), record[1].astype(jnp.float32)], axis=1)
    for copy in copies:
        copy.wait()
    whiten_rows(windows, starts, live, wide, band, places, out)


def whiten_all_kernel(windows, starts, live, record, taps, *refs):
    sources, out, places, arrivals = refs[:6], refs[6], refs[7:13], refs[13]
    copies = start_tables(sources, places, arrivals)
    band = band_rows(taps[...])
    wide = record[...].astype(jnp.float32)
    for copy in copies:
        copy.wait()
    whiten_rows(windows, starts, live, wide, band, places, out)


def whiten_rows(windows, starts, live, wide, band, places, out):
    forward_high, forward_low, inverse_high, inverse_low, mean_table, edge = places
    channels, length = wide.shape
    pieces = []
    for window_at in range(windows):
        start = starts[window_at]
        rolled = pltpu.roll(wide, lax.rem(length - start, length), 1).astype(jnp.bfloat16)
        parts = [
            lax.dot_general(
                rolled[:, at * BLOCK * DECIM : at * BLOCK * DECIM + REACH],
                band,
                (((1,), (1,)), ((), ())),
                preferred_element_type=jnp.float32,
            )
            for at in range(NS // BLOCK)
        ]
        pieces.append(jnp.concatenate(parts, axis=1))
    decimated = jnp.concatenate(pieces, axis=0)
    row_at = lax.broadcasted_iota(jnp.int32, (channels, NS), 0)
    kept = jnp.zeros((channels, NS), jnp.float32)
    for channel in range(channels):
        kept = jnp.where(row_at == channel, live[channel].astype(jnp.float32), kept)
    first, second = decimated[:, :FOLD], decimated[:, FOLD:]
    even = split_dot(first + second, forward_high[0], forward_low[0])
    odd = split_dot(first - second, forward_high[1], forward_low[1])
    quarter = NS // 4
    real_part = jnp.concatenate([even[:, :quarter], odd[:, :quarter]], axis=1)
    imag_part = jnp.concatenate([even[:, quarter:], odd[:, quarter:]], axis=1)
    at_zero = lax.broadcasted_iota(jnp.int32, real_part.shape, 1) == 0
    amplitude = jnp.sqrt(real_part * real_part + jnp.where(at_zero, 0.0, imag_part * imag_part))
    top = jnp.abs(imag_part[:, 0:1])
    amp_high = amplitude.astype(jnp.bfloat16)
    amp_low = (amplitude - amp_high.astype(jnp.float32)).astype(jnp.bfloat16)
    summed = dot(amp_high, mean_table[...]) + dot(amp_low, mean_table[...]) + top * edge[0:1, :]
    summed_top = jnp.sum(amplitude * edge[1:2, :], axis=1, keepdims=True) + top
    width = 2 * HALF + 1
    scale = 1.0 / (summed * (1.0 / width) + EPSILON)
    scale_top = 1.0 / (summed_top * (1.0 / width) + EPSILON)
    white_real = real_part * scale
    white_imag = imag_part * jnp.where(at_zero, scale_top, scale)
    white_even = jnp.concatenate([white_real[:, :quarter], white_imag[:, :quarter]], axis=1)
    white_odd = jnp.concatenate([white_real[:, quarter:], white_imag[:, quarter:]], axis=1)
    from_even = split_dot(white_even, inverse_high[0], inverse_low[0])
    from_odd = split_dot(white_odd, inverse_high[1], inverse_low[1])
    series = jnp.concatenate([from_even + from_odd, from_even - from_odd], axis=1)
    for window_at in range(windows):
        rows = series[window_at * channels : (window_at + 1) * channels]
        out[window_at] = (rows * kept).astype(jnp.bfloat16)


def lag_sums(place, gathered, turned, lagged):
    blocks, windows, channels, _ = gathered.shape
    sources = channels // STRIDE
    chan_at = place[1]
    source_block = chan_at // STRIDE * STRIDE
    source_part = lax.rem(chan_at, STRIDE)
    total = None
    for window_at in range(windows):
        rows = gathered[source_block, window_at].astype(jnp.float32)
        chosen = jnp.where(source_part == 0, rows[:sources], rows[sources:])
        for row in range(8):
            turned[:, row, :] = pltpu.roll(chosen, (NS - row) % NS, 1)
        for source in range(sources):
            base = turned[source]
            for first in range(0, LAG_ROWS, 16):
                pair = [pltpu.roll(base, (LAGS // 2 - first - 8 * at) % NS, 1) for at in range(2)]
                lagged[source, first : first + 16, :] = jnp.concatenate(pair, axis=0).astype(jnp.bfloat16)
        term = lax.dot_general(
            lagged[...].reshape(sources * LAG_ROWS, NS),
            gathered[:, window_at].reshape(blocks * channels, NS),
            (((1,), (1,)), ((), ())),
            preferred_element_type=jnp.float32,
        )
        total = term if total is None else total + term
    return total


def gather_corr_kernel(scale, series, out, held, turned, lagged, outgoing, arrived,
                       sent, landed, swap_sent, swap_landed):
    blocks, windows, channels, _ = held.shape
    sources = channels // STRIDE
    layers = blocks // 4
    win_at = lax.axis_index("win")
    me = lax.axis_index("chan")
    layer, core = me // 4, lax.rem(me, 2)
    lane = lax.rem(me, 4)
    beside = layer * 4 + lax.rem(lane + 2, 4)
    twin = me + 1 - 2 * core
    twin_lane = lane + 1 - 2 * core
    other_lane = lax.rem(lane + 2, 4)
    partner = 1 - win_at
    above, below = me + 4, me - 4
    has_above, has_below = layer < layers - 1, layer > 0
    mesh_id = pl.DeviceIdType.MESH

    barrier = pltpu.get_barrier_semaphore()
    pl.semaphore_signal(barrier, inc=1, device_id=(win_at, beside), device_id_type=mesh_id)
    pl.semaphore_signal(barrier, inc=1, device_id=(win_at, twin), device_id_type=mesh_id)
    pl.semaphore_signal(barrier, inc=1, device_id=(partner, me), device_id_type=mesh_id)

    @pl.when(has_above)
    def _():
        pl.semaphore_signal(barrier, inc=1, device_id=(win_at, above), device_id_type=mesh_id)

    @pl.when(has_below)
    def _():
        pl.semaphore_signal(barrier, inc=1, device_id=(win_at, below), device_id_type=mesh_id)

    held[me] = series[...]
    pl.semaphore_wait(barrier, 3 + has_above.astype(jnp.int32) + has_below.astype(jnp.int32))

    chunk = windows // CHUNKS

    def move(way, block, part, target):
        span = held.at[block, pl.ds(part * chunk, chunk)]
        return pltpu.make_async_remote_copy(
            src_ref=span,
            dst_ref=span,
            send_sem=sent.at[way, block, part],
            recv_sem=landed.at[block, part],
            device_id=(win_at, target),
            device_id_type=mesh_id,
        )

    def up(block, part):
        return move(0, block, part, above)

    def down(block, part):
        return move(1, block, part, below)

    def across(block, part):
        return move(2, block, part, beside)

    def over(block, part):
        return move(3, block, part, twin)

    def await_block(block, part):
        across(block, part).wait_recv()

    def when(condition, action):
        @pl.when(condition)
        def _():
            action()

    for part in range(CHUNKS):
        when(has_above, lambda: up(me, part).start())
        when(has_below, lambda: down(me, part).start())
        across(me, part).start()
        over(me, part).start()

    source_block = me // STRIDE * STRIDE
    source_part = lax.rem(me, STRIDE)

    def build(window_at):
        rows = held[source_block, window_at].astype(jnp.float32)
        chosen = jnp.where(source_part == 0, rows[:sources], rows[sources:])
        for row in range(8):
            turned[:, row, :] = pltpu.roll(chosen, (NS - row) % NS, 1)

        def build_source(source, carry):
            base = turned[source]
            for first in range(0, LAG_ROWS, 16):
                pair = [pltpu.roll(base, (LAGS // 2 - first - 8 * at) % NS, 1) for at in range(2)]
                lagged[window_at, source, first : first + 16, :] = jnp.concatenate(pair, axis=0).astype(jnp.bfloat16)
            return carry

        lax.fori_loop(0, sources, build_source, 0)

    def pass_lane(distance, part):
        for sign in (-1, 1):
            origin = layer + sign * distance
            block = me + 4 * sign * distance
            exists = (origin >= 0) if sign < 0 else (origin < layers)
            further = has_above if sign < 0 else has_below

            def relay():
                await_block(block, part)
                when(further, lambda: (up if sign < 0 else down)(block, part).start())
                across(block, part).start()
                over(block, part).start()

            when(exists, relay)

    def pass_beside(distance, part):
        for sign in (-1, 1) if distance else (1,):
            origin = layer + sign * distance
            block = origin * 4 + other_lane
            exists = (origin >= 0) if sign < 0 else (origin < layers)

            def relay():
                await_block(block, part)
                over(block, part).start()

            when(exists, relay)

    to_build = list(range(windows))
    for part in range(CHUNKS):
        await_block(twin, part)
    build(to_build.pop(0))
    for distance in range(1, layers):
        for part in range(CHUNKS):
            pass_lane(distance, part)
            if to_build:
                build(to_build.pop(0))
            pass_beside(distance - 1, part)
    while to_build:
        build(to_build.pop(0))
    half_blocks = blocks // 2

    def window_sums(half, window_at):
        return lax.dot_general(
            lagged[window_at].reshape(sources * LAG_ROWS, NS),
            held[pl.ds(half * half_blocks, half_blocks), window_at].reshape(half_blocks * channels, NS),
            (((1,), (1,)), ((), ())),
            preferred_element_type=jnp.float32,
        )

    for part in range(CHUNKS):
        pass_beside(layers - 1, part)
    partial = None
    for part in range(CHUNKS):
        for at in range(layers):
            await_block(at * 4 + lax.rem(twin_lane + 2, 4), part)
            mine = at * 4 + twin_lane
            when(mine != twin, lambda: await_block(mine, part))
        for window_at in range(part * chunk, (part + 1) * chunk):
            term = window_sums(partner, window_at)
            partial = term if partial is None else partial + term

    def own_sums():
        total = None
        for window_at in range(windows):
            term = window_sums(win_at, window_at)
            total = term if total is None else total + term
        return total * scale

    outgoing[...] = (partial * scale).astype(jnp.bfloat16).reshape(outgoing.shape)
    swap = pltpu.make_async_remote_copy(
        src_ref=outgoing,
        dst_ref=arrived,
        send_sem=swap_sent,
        recv_sem=swap_landed,
        device_id=(partner, me),
        device_id_type=mesh_id,
    )
    swap.start()
    kept = own_sums().reshape(outgoing.shape)
    swap.wait()
    total = kept + arrived[...].astype(jnp.float32)
    for source in range(sources):
        out[source] = total[source, :LAGS]

    for at in range(layers):
        block = at * 4 + lane
        for part in range(CHUNKS):
            when(jnp.logical_and(has_above, at <= layer), lambda: up(block, part).wait_send())
            when(jnp.logical_and(has_below, at >= layer), lambda: down(block, part).wait_send())
            across(block, part).wait_send()
            over(block, part).wait_send()
            over(at * 4 + other_lane, part).wait_send()


def corr_all_kernel(scale, place, gathered, own, turned, lagged):
    total = lag_sums(place, gathered, turned, lagged) * scale
    for source in range(own.shape[0]):
        own[source] = total[source * LAG_ROWS : source * LAG_ROWS + LAGS]


def whole_in_vmem(count):
    return [pl.BlockSpec(memory_space=pltpu.VMEM)] * count


def local(tables, strain_raw, fir_taps, live_mask, window_start):
    channels = strain_raw.shape[0]
    windows = window_start.shape[0]
    groups = lax.axis_size("win")
    blocks = lax.axis_size("chan")
    win_at = lax.axis_index("win")
    chan_at = lax.axis_index("chan")
    params = pltpu.CompilerParams(vmem_limit_bytes=VMEM_LIMIT)
    smem = pl.BlockSpec(memory_space=pltpu.SMEM)
    places = [pltpu.VMEM(table.shape, table.dtype) for table in tables]
    taps = fir_taps.astype(jnp.float32)[None, :]
    whiten_specs = dict(
        out_shape=jax.ShapeDtypeStruct((windows, channels, NS), jnp.bfloat16),
        in_specs=[smem, smem] + whole_in_vmem(2) + [pl.BlockSpec(memory_space=pltpu.HBM)] * len(tables),
        out_specs=pl.BlockSpec(memory_space=pltpu.VMEM),
        name="whiten",
    )
    if groups == 2:
        series = pl.pallas_call(
            lambda *refs: whiten_pair_kernel(windows, *refs),
            scratch_shapes=[pltpu.VMEM((2,) + strain_raw.shape, strain_raw.dtype)]
            + places
            + [pltpu.SemaphoreType.DMA((len(tables),)), pltpu.SemaphoreType.DMA, pltpu.SemaphoreType.DMA],
            compiler_params=pltpu.CompilerParams(
                vmem_limit_bytes=VMEM_LIMIT, collective_id=1, has_side_effects=True
            ),
            **whiten_specs,
        )(window_start, live_mask, strain_raw, taps, *tables)
    else:
        record = lax.all_gather(strain_raw, "win", axis=1, tiled=True)
        series = pl.pallas_call(
            lambda *refs: whiten_all_kernel(windows, *refs),
            scratch_shapes=places + [pltpu.SemaphoreType.DMA((len(tables),))],
            compiler_params=params,
            **whiten_specs,
        )(window_start, live_mask, record, taps, *tables)
    scale = 1.0 / (math.sqrt(NS) * math.sqrt(windows * groups))
    sources = channels // STRIDE
    total = blocks * channels
    if groups == 2 and blocks == 16:
        return pl.pallas_call(
            lambda *refs: gather_corr_kernel(scale, *refs),
            out_shape=jax.ShapeDtypeStruct((sources, LAGS, total // 2), jnp.float32),
            in_specs=whole_in_vmem(1),
            out_specs=pl.BlockSpec(memory_space=pltpu.VMEM),
            scratch_shapes=[
                pltpu.VMEM((blocks, windows, channels, NS), jnp.bfloat16),
                pltpu.VMEM((sources, 8, NS), jnp.float32),
                pltpu.VMEM((windows, sources, LAG_ROWS, NS), jnp.bfloat16),
                pltpu.VMEM((sources, LAG_ROWS, total // 2), jnp.bfloat16),
                pltpu.VMEM((sources, LAG_ROWS, total // 2), jnp.bfloat16),
                pltpu.SemaphoreType.DMA((4, blocks, CHUNKS)),
                pltpu.SemaphoreType.DMA((blocks, CHUNKS)),
                pltpu.SemaphoreType.DMA,
                pltpu.SemaphoreType.DMA,
            ],
            compiler_params=pltpu.CompilerParams(
                vmem_limit_bytes=VMEM_LIMIT, collective_id=0, has_side_effects=True
            ),
            name="gather_correlate",
        )(series)
    gathered = lax.all_gather(series, "chan", axis=0, tiled=False)
    place = jnp.stack([win_at, chan_at]).astype(jnp.int32)
    scratch = [
        pltpu.VMEM((sources, 8, NS), jnp.float32),
        pltpu.VMEM((sources, LAG_ROWS, NS), jnp.bfloat16),
    ]
    own = pl.pallas_call(
        lambda *refs: corr_all_kernel(scale, *refs),
        out_shape=jax.ShapeDtypeStruct((sources, LAGS, total), jnp.float32),
        in_specs=[smem] + whole_in_vmem(1),
        out_specs=pl.BlockSpec(memory_space=pltpu.VMEM),
        scratch_shapes=scratch,
        compiler_params=params,
        name="correlate",
    )(place, gathered)
    return lax.psum_scatter(own, "win", scatter_dimension=2, tiled=True)


def solution(mesh):
    in_specs = (P("chan", "win"), P(), P("chan"), P("win"))
    out_specs = P("chan", None, "win")

    def run(strain_raw, fir_taps, live_mask, window_start):
        tables = [jnp.asarray(table) for table in build_tables()]
        mapped = jax.shard_map(
            lambda tables, *args: local(tables, *args),
            mesh=mesh,
            in_specs=(P(),) + in_specs,
            out_specs=out_specs,
            check_vma=False,
        )
        return mapped(tables, strain_raw, fir_taps, live_mask, window_start)

    return run
```

```python
import math

import jax
import jax.numpy as jnp
import ml_dtypes
import numpy as np
from jax import lax
from jax.experimental import pallas as pl
from jax.experimental.pallas import tpu as pltpu
from jax.sharding import PartitionSpec as P

NS = 1024
DECIM = 4
TAPS = 128
HALF = 32
LAGS = 101
STRIDE = 2
EPSILON = 1e-06

FOLD = NS // 2
BLOCK = 128
REACH = BLOCK * DECIM + TAPS
LAG_ROWS = 112
CHUNKS = 2
VMEM_LIMIT = 60 * 1024 * 1024
CORR_VMEM_LIMIT = 40 * 1024 * 1024


def split_table(table):
    high = table.astype(ml_dtypes.bfloat16)
    low = (table - high.astype(np.float64)).astype(ml_dtypes.bfloat16)
    return high, low


def build_tables():
    time_at = np.arange(FOLD)
    forward = []
    inverse = []
    for parity in range(2):
        bins = 2 * np.arange(NS // 4) + parity
        angle = 2.0 * np.pi * ((time_at[:, None] * bins[None, :]) % NS) / NS
        cosine = np.cos(angle)
        sine = -np.sin(angle)
        weight = np.full((2 * bins.size,), 2.0 / math.sqrt(NS))
        if parity == 0:
            sine[:, 0] = np.cos(np.pi * time_at)
            weight[0] = 1.0 / math.sqrt(NS)
            weight[bins.size] = 1.0 / math.sqrt(NS)
        table = np.concatenate([cosine, sine], axis=1)
        forward.append(table)
        inverse.append((table * weight[None, :]).T)
    order = np.concatenate([np.arange(0, FOLD, 2), np.arange(1, FOLD, 2), [FOLD]])
    place = np.zeros((FOLD + 1,), np.int64)
    place[order] = np.arange(FOLD + 1)
    counts = np.zeros((FOLD + 1, FOLD + 1))
    for column, bin_at in enumerate(order):
        for offset in range(-HALF, HALF + 1):
            seen = (bin_at + offset) % NS
            counts[place[min(seen, NS - seen)], column] += 1.0
    mean_table = counts[:FOLD, :FOLD].astype(ml_dtypes.bfloat16)
    edge = np.zeros((8, FOLD), np.float32)
    edge[0] = counts[FOLD, :FOLD]
    edge[1] = counts[:FOLD, FOLD]
    forward_high, forward_low = split_table(np.stack(forward))
    inverse_high, inverse_low = split_table(np.stack(inverse))
    return forward_high, forward_low, inverse_high, inverse_low, mean_table, edge


def dot(left, right):
    return jnp.dot(left, right, preferred_element_type=jnp.float32)


def split_dot(value, high, low):
    rows = value.shape[0]
    value_high = value.astype(jnp.bfloat16)
    value_low = (value - value_high.astype(jnp.float32)).astype(jnp.bfloat16)
    both = dot(jnp.concatenate([value_high, value_low], axis=0), high)
    return both[:rows] + both[rows:] + dot(value_high, low)


def start_tables(sources, places, arrivals):
    copies = [pltpu.make_async_copy(source, place, arrivals.at[at])
              for at, (source, place) in enumerate(zip(sources, places))]
    for copy in copies:
        copy.start()
    return copies


def band_rows(taps):
    rows = jnp.concatenate([taps, jnp.zeros((1, REACH - TAPS), jnp.float32)], axis=1)
    rows = jnp.broadcast_to(rows, (BLOCK, REACH))
    row_at = lax.broadcasted_iota(jnp.int32, (BLOCK, REACH), 0)
    step = 1
    while step < BLOCK:
        rows = jnp.where(row_at // step % 2 == 1, pltpu.roll(rows, step * DECIM, 1), rows)
        step *= 2
    return rows.astype(jnp.bfloat16)


def whiten_pair_kernel(windows, starts, live, strain, taps, *refs):
    sources, out, record = refs[:6], refs[6], refs[7]
    places, (arrivals, sent, landed) = refs[8:14], refs[14:]
    copies = start_tables(sources, places, arrivals)
    win_at = lax.axis_index("win")
    partner = (1 - win_at, lax.axis_index("chan"))
    barrier = pltpu.get_barrier_semaphore()
    pl.semaphore_signal(barrier, inc=1, device_id=partner, device_id_type=pl.DeviceIdType.MESH)
    pl.semaphore_wait(barrier, 1)
    swap = pltpu.make_async_remote_copy(
        src_ref=strain,
        dst_ref=record.at[win_at],
        send_sem=sent,
        recv_sem=landed,
        device_id=partner,
        device_id_type=pl.DeviceIdType.MESH,
    )
    swap.start()
    record[win_at] = strain[...]
    band = band_rows(taps[...])
    swap.wait()
    wide = jnp.concatenate([record[0].astype(jnp.float32), record[1].astype(jnp.float32)], axis=1)
    for copy in copies:
        copy.wait()
    whiten_rows(windows, starts, live, wide, band, places, out)


def whiten_all_kernel(windows, starts, live, record, taps, *refs):
    sources, out, places, arrivals = refs[:6], refs[6], refs[7:13], refs[13]
    copies = start_tables(sources, places, arrivals)
    band = band_rows(taps[...])
    wide = record[...].astype(jnp.float32)
    for copy in copies:
        copy.wait()
    whiten_rows(windows, starts, live, wide, band, places, out)


def whiten_rows(windows, starts, live, wide, band, places, out):
    forward_high, forward_low, inverse_high, inverse_low, mean_table, edge = places
    channels, length = wide.shape
    pieces = []
    for window_at in range(windows):
        start = starts[window_at]
        rolled = pltpu.roll(wide, lax.rem(length - start, length), 1).astype(jnp.bfloat16)
        parts = [
            lax.dot_general(
                rolled[:, at * BLOCK * DECIM : at * BLOCK * DECIM + REACH],
                band,
                (((1,), (1,)), ((), ())),
                preferred_element_type=jnp.float32,
            )
            for at in range(NS // BLOCK)
        ]
        pieces.append(jnp.concatenate(parts, axis=1))
    decimated = jnp.concatenate(pieces, axis=0)
    row_at = lax.broadcasted_iota(jnp.int32, (channels, NS), 0)
    kept = jnp.zeros((channels, NS), jnp.float32)
    for channel in range(channels):
        kept = jnp.where(row_at == channel, live[channel].astype(jnp.float32), kept)
    first, second = decimated[:, :FOLD], decimated[:, FOLD:]
    even = split_dot(first + second, forward_high[0], forward_low[0])
    odd = split_dot(first - second, forward_high[1], forward_low[1])
    quarter = NS // 4
    real_part = jnp.concatenate([even[:, :quarter], odd[:, :quarter]], axis=1)
    imag_part = jnp.concatenate([even[:, quarter:], odd[:, quarter:]], axis=1)
    at_zero = lax.broadcasted_iota(jnp.int32, real_part.shape, 1) == 0
    amplitude = jnp.sqrt(real_part * real_part + jnp.where(at_zero, 0.0, imag_part * imag_part))
    top = jnp.abs(imag_part[:, 0:1])
    amp_high = amplitude.astype(jnp.bfloat16)
    amp_low = (amplitude - amp_high.astype(jnp.float32)).astype(jnp.bfloat16)
    summed = dot(amp_high, mean_table[...]) + dot(amp_low, mean_table[...]) + top * edge[0:1, :]
    summed_top = jnp.sum(amplitude * edge[1:2, :], axis=1, keepdims=True) + top
    width = 2 * HALF + 1
    scale = 1.0 / (summed * (1.0 / width) + EPSILON)
    scale_top = 1.0 / (summed_top * (1.0 / width) + EPSILON)
    white_real = real_part * scale
    white_imag = imag_part * jnp.where(at_zero, scale_top, scale)
    white_even = jnp.concatenate([white_real[:, :quarter], white_imag[:, :quarter]], axis=1)
    white_odd = jnp.concatenate([white_real[:, quarter:], white_imag[:, quarter:]], axis=1)
    from_even = split_dot(white_even, inverse_high[0], inverse_low[0])
    from_odd = split_dot(white_odd, inverse_high[1], inverse_low[1])
    series = jnp.concatenate([from_even + from_odd, from_even - from_odd], axis=1)
    for window_at in range(windows):
        rows = series[window_at * channels : (window_at + 1) * channels]
        out[window_at] = (rows * kept).astype(jnp.bfloat16)


def lag_sums(place, gathered, turned, lagged):
    blocks, windows, channels, _ = gathered.shape
    sources = channels // STRIDE
    chan_at = place[1]
    source_block = chan_at // STRIDE * STRIDE
    source_part = lax.rem(chan_at, STRIDE)
    total = None
    for window_at in range(windows):
        rows = gathered[source_block, window_at].astype(jnp.float32)
        chosen = jnp.where(source_part == 0, rows[:sources], rows[sources:])
        for row in range(8):
            turned[:, row, :] = pltpu.roll(chosen, (NS - row) % NS, 1)
        for source in range(sources):
            base = turned[source]
            for first in range(0, LAG_ROWS, 16):
                pair = [pltpu.roll(base, (LAGS // 2 - first - 8 * at) % NS, 1) for at in range(2)]
                lagged[source, first : first + 16, :] = jnp.concatenate(pair, axis=0).astype(jnp.bfloat16)
        term = lax.dot_general(
            lagged[...].reshape(sources * LAG_ROWS, NS),
            gathered[:, window_at].reshape(blocks * channels, NS),
            (((1,), (1,)), ((), ())),
            preferred_element_type=jnp.float32,
        )
        total = term if total is None else total + term
    return total


def gather_corr_kernel(scale, series, out, held, turned, lagged, outgoing, arrived,
                       sent, landed, swap_sent, swap_landed):
    blocks, windows, channels, _ = held.shape
    sources = channels // STRIDE
    layers = blocks // 4
    win_at = lax.axis_index("win")
    me = lax.axis_index("chan")
    layer, core = me // 4, lax.rem(me, 2)
    lane = lax.rem(me, 4)
    beside = layer * 4 + lax.rem(lane + 2, 4)
    twin = me + 1 - 2 * core
    twin_lane = lane + 1 - 2 * core
    other_lane = lax.rem(lane + 2, 4)
    partner = 1 - win_at
    above, below = me + 4, me - 4
    has_above, has_below = layer < layers - 1, layer > 0
    mesh_id = pl.DeviceIdType.MESH

    barrier = pltpu.get_barrier_semaphore()
    pl.semaphore_signal(barrier, inc=1, device_id=(win_at, beside), device_id_type=mesh_id)
    pl.semaphore_signal(barrier, inc=1, device_id=(win_at, twin), device_id_type=mesh_id)
    pl.semaphore_signal(barrier, inc=1, device_id=(partner, me), device_id_type=mesh_id)

    @pl.when(has_above)
    def _():
        pl.semaphore_signal(barrier, inc=1, device_id=(win_at, above), device_id_type=mesh_id)

    @pl.when(has_below)
    def _():
        pl.semaphore_signal(barrier, inc=1, device_id=(win_at, below), device_id_type=mesh_id)

    held[me] = series[...]
    pl.semaphore_wait(barrier, 3 + has_above.astype(jnp.int32) + has_below.astype(jnp.int32))

    chunk = windows // CHUNKS

    def move(way, block, part, target):
        span = held.at[block, pl.ds(part * chunk, chunk)]
        return pltpu.make_async_remote_copy(
            src_ref=span,
            dst_ref=span,
            send_sem=sent.at[way, block, part],
            recv_sem=landed.at[block, part],
            device_id=(win_at, target),
            device_id_type=mesh_id,
        )

    def up(block, part):
        return move(0, block, part, above)

    def down(block, part):
        return move(1, block, part, below)

    def across(block, part):
        return move(2, block, part, beside)

    def over(block, part):
        return move(3, block, part, twin)

    def await_block(block, part):
        across(block, part).wait_recv()

    def when(condition, action):
        @pl.when(condition)
        def _():
            action()

    for part in range(CHUNKS):
        when(has_above, lambda: up(me, part).start())
        when(has_below, lambda: down(me, part).start())
        across(me, part).start()
        over(me, part).start()

    source_block = me // STRIDE * STRIDE
    source_part = lax.rem(me, STRIDE)

    def build(window_at):
        rows = held[source_block, window_at].astype(jnp.float32)
        chosen = jnp.where(source_part == 0, rows[:sources], rows[sources:])
        for row in range(8):
            turned[:, row, :] = pltpu.roll(chosen, (NS - row) % NS, 1)

        def build_source(source, carry):
            base = turned[source]
            for first in range(0, LAG_ROWS, 16):
                pair = [pltpu.roll(base, (LAGS // 2 - first - 8 * at) % NS, 1) for at in range(2)]
                lagged[window_at, source, first : first + 16, :] = jnp.concatenate(pair, axis=0).astype(jnp.bfloat16)
            return carry

        lax.fori_loop(0, sources, build_source, 0)

    def pass_lane(distance, part):
        for sign in (-1, 1):
            origin = layer + sign * distance
            block = me + 4 * sign * distance
            exists = (origin >= 0) if sign < 0 else (origin < layers)
            further = has_above if sign < 0 else has_below

            def relay():
                await_block(block, part)
                when(further, lambda: (up if sign < 0 else down)(block, part).start())
                across(block, part).start()
                over(block, part).start()

            when(exists, relay)

    def pass_beside(distance, part):
        for sign in (-1, 1) if distance else (1,):
            origin = layer + sign * distance
            block = origin * 4 + other_lane
            exists = (origin >= 0) if sign < 0 else (origin < layers)

            def relay():
                await_block(block, part)
                over(block, part).start()

            when(exists, relay)

    to_build = list(range(windows))
    for part in range(CHUNKS):
        await_block(twin, part)
    build(to_build.pop(0))
    for distance in range(1, layers):
        for part in range(CHUNKS):
            pass_lane(distance, part)
            if to_build:
                build(to_build.pop(0))
            pass_beside(distance - 1, part)
    while to_build:
        build(to_build.pop(0))
    half_blocks = blocks // 2

    def window_sums(half, window_at):
        return lax.dot_general(
            lagged[window_at].reshape(sources * LAG_ROWS, NS),
            held[pl.ds(half * half_blocks, half_blocks), window_at].reshape(half_blocks * channels, NS),
            (((1,), (1,)), ((), ())),
            preferred_element_type=jnp.float32,
        )

    for part in range(CHUNKS):
        pass_beside(layers - 1, part)
    partial = None
    for part in range(CHUNKS):
        for at in range(layers):
            await_block(at * 4 + lax.rem(twin_lane + 2, 4), part)
            mine = at * 4 + twin_lane
            when(mine != twin, lambda: await_block(mine, part))
        for window_at in range(part * chunk, (part + 1) * chunk):
            term = window_sums(partner, window_at)
            partial = term if partial is None else partial + term

    def own_sums():
        total = None
        for window_at in range(windows):
            term = window_sums(win_at, window_at)
            total = term if total is None else total + term
        return total * scale

    outgoing[...] = (partial * scale).astype(jnp.bfloat16).reshape(outgoing.shape)
    swap = pltpu.make_async_remote_copy(
        src_ref=outgoing,
        dst_ref=arrived,
        send_sem=swap_sent,
        recv_sem=swap_landed,
        device_id=(partner, me),
        device_id_type=mesh_id,
    )
    swap.start()
    kept = own_sums().reshape(outgoing.shape)
    swap.wait()
    total = kept + arrived[...].astype(jnp.float32)
    for source in range(sources):
        out[source] = total[source, :LAGS]

    for at in range(layers):
        block = at * 4 + lane
        for part in range(CHUNKS):
            when(jnp.logical_and(has_above, at <= layer), lambda: up(block, part).wait_send())
            when(jnp.logical_and(has_below, at >= layer), lambda: down(block, part).wait_send())
            across(block, part).wait_send()
            over(block, part).wait_send()
            over(at * 4 + other_lane, part).wait_send()


def corr_all_kernel(scale, place, gathered, own, turned, lagged):
    total = lag_sums(place, gathered, turned, lagged) * scale
    for source in range(own.shape[0]):
        own[source] = total[source * LAG_ROWS : source * LAG_ROWS + LAGS]


def whole_in_vmem(count):
    return [pl.BlockSpec(memory_space=pltpu.VMEM)] * count


def local(tables, strain_raw, fir_taps, live_mask, window_start):
    channels = strain_raw.shape[0]
    windows = window_start.shape[0]
    groups = lax.axis_size("win")
    blocks = lax.axis_size("chan")
    win_at = lax.axis_index("win")
    chan_at = lax.axis_index("chan")
    params = pltpu.CompilerParams(vmem_limit_bytes=VMEM_LIMIT)
    smem = pl.BlockSpec(memory_space=pltpu.SMEM)
    places = [pltpu.VMEM(table.shape, table.dtype) for table in tables]
    taps = fir_taps.astype(jnp.float32)[None, :]
    whiten_specs = dict(
        out_shape=jax.ShapeDtypeStruct((windows, channels, NS), jnp.bfloat16),
        in_specs=[smem, smem] + whole_in_vmem(2) + [pl.BlockSpec(memory_space=pltpu.HBM)] * len(tables),
        out_specs=pl.BlockSpec(memory_space=pltpu.VMEM),
        name="whiten",
    )
    if groups == 2:
        series = pl.pallas_call(
            lambda *refs: whiten_pair_kernel(windows, *refs),
            scratch_shapes=[pltpu.VMEM((2,) + strain_raw.shape, strain_raw.dtype)]
            + places
            + [pltpu.SemaphoreType.DMA((len(tables),)), pltpu.SemaphoreType.DMA, pltpu.SemaphoreType.DMA],
            compiler_params=pltpu.CompilerParams(
                vmem_limit_bytes=VMEM_LIMIT, collective_id=1, has_side_effects=True
            ),
            **whiten_specs,
        )(window_start, live_mask, strain_raw, taps, *tables)
    else:
        record = lax.all_gather(strain_raw, "win", axis=1, tiled=True)
        series = pl.pallas_call(
            lambda *refs: whiten_all_kernel(windows, *refs),
            scratch_shapes=places + [pltpu.SemaphoreType.DMA((len(tables),))],
            compiler_params=params,
            **whiten_specs,
        )(window_start, live_mask, record, taps, *tables)
    scale = 1.0 / (math.sqrt(NS) * math.sqrt(windows * groups))
    sources = channels // STRIDE
    total = blocks * channels
    if groups == 2 and blocks == 16:
        return pl.pallas_call(
            lambda *refs: gather_corr_kernel(scale, *refs),
            out_shape=jax.ShapeDtypeStruct((sources, LAGS, total // 2), jnp.float32),
            in_specs=whole_in_vmem(1),
            out_specs=pl.BlockSpec(memory_space=pltpu.VMEM),
            scratch_shapes=[
                pltpu.VMEM((blocks, windows, channels, NS), jnp.bfloat16),
                pltpu.VMEM((sources, 8, NS), jnp.float32),
                pltpu.VMEM((windows, sources, LAG_ROWS, NS), jnp.bfloat16),
                pltpu.VMEM((sources, LAG_ROWS, total // 2), jnp.bfloat16),
                pltpu.VMEM((sources, LAG_ROWS, total // 2), jnp.bfloat16),
                pltpu.SemaphoreType.DMA((4, blocks, CHUNKS)),
                pltpu.SemaphoreType.DMA((blocks, CHUNKS)),
                pltpu.SemaphoreType.DMA,
                pltpu.SemaphoreType.DMA,
            ],
            compiler_params=pltpu.CompilerParams(
                vmem_limit_bytes=CORR_VMEM_LIMIT, collective_id=0, has_side_effects=True
            ),
            name="gather_correlate",
        )(series)
    gathered = lax.all_gather(series, "chan", axis=0, tiled=False)
    place = jnp.stack([win_at, chan_at]).astype(jnp.int32)
    scratch = [
        pltpu.VMEM((sources, 8, NS), jnp.float32),
        pltpu.VMEM((sources, LAG_ROWS, NS), jnp.bfloat16),
    ]
    own = pl.pallas_call(
        lambda *refs: corr_all_kernel(scale, *refs),
        out_shape=jax.ShapeDtypeStruct((sources, LAGS, total), jnp.float32),
        in_specs=[smem] + whole_in_vmem(1),
        out_specs=pl.BlockSpec(memory_space=pltpu.VMEM),
        scratch_shapes=scratch,
        compiler_params=params,
        name="correlate",
    )(place, gathered)
    return lax.psum_scatter(own, "win", scatter_dimension=2, tiled=True)


def solution(mesh):
    in_specs = (P("chan", "win"), P(), P("chan"), P("win"))
    out_specs = P("chan", None, "win")

    def run(strain_raw, fir_taps, live_mask, window_start):
        tables = [jnp.asarray(table) for table in build_tables()]
        mapped = jax.shard_map(
            lambda tables, *args: local(tables, *args),
            mesh=mesh,
            in_specs=(P(),) + in_specs,
            out_specs=out_specs,
            check_vma=False,
        )
        return mapped(tables, strain_raw, fir_taps, live_mask, window_start)

    return run
```

```python
import math

import jax
import jax.numpy as jnp
import ml_dtypes
import numpy as np
from jax import lax
from jax.experimental import pallas as pl
from jax.experimental.pallas import tpu as pltpu
from jax.sharding import PartitionSpec as P

NS = 1024
DECIM = 4
TAPS = 128
HALF = 32
LAGS = 101
STRIDE = 2
EPSILON = 1e-06

FOLD = NS // 2
BLOCK = 128
REACH = BLOCK * DECIM + TAPS
LAG_ROWS = 112
CHUNKS = 4
VMEM_LIMIT = 60 * 1024 * 1024
CORR_VMEM_LIMIT = 40 * 1024 * 1024


def split_table(table):
    high = table.astype(ml_dtypes.bfloat16)
    low = (table - high.astype(np.float64)).astype(ml_dtypes.bfloat16)
    return high, low


def build_tables():
    time_at = np.arange(FOLD)
    forward = []
    inverse = []
    for parity in range(2):
        bins = 2 * np.arange(NS // 4) + parity
        angle = 2.0 * np.pi * ((time_at[:, None] * bins[None, :]) % NS) / NS
        cosine = np.cos(angle)
        sine = -np.sin(angle)
        weight = np.full((2 * bins.size,), 2.0 / math.sqrt(NS))
        if parity == 0:
            sine[:, 0] = np.cos(np.pi * time_at)
            weight[0] = 1.0 / math.sqrt(NS)
            weight[bins.size] = 1.0 / math.sqrt(NS)
        table = np.concatenate([cosine, sine], axis=1)
        forward.append(table)
        inverse.append((table * weight[None, :]).T)
    order = np.concatenate([np.arange(0, FOLD, 2), np.arange(1, FOLD, 2), [FOLD]])
    place = np.zeros((FOLD + 1,), np.int64)
    place[order] = np.arange(FOLD + 1)
    counts = np.zeros((FOLD + 1, FOLD + 1))
    for column, bin_at in enumerate(order):
        for offset in range(-HALF, HALF + 1):
            seen = (bin_at + offset) % NS
            counts[place[min(seen, NS - seen)], column] += 1.0
    mean_table = counts[:FOLD, :FOLD].astype(ml_dtypes.bfloat16)
    edge = np.zeros((8, FOLD), np.float32)
    edge[0] = counts[FOLD, :FOLD]
    edge[1] = counts[:FOLD, FOLD]
    forward_high, forward_low = split_table(np.stack(forward))
    inverse_high, inverse_low = split_table(np.stack(inverse))
    return forward_high, forward_low, inverse_high, inverse_low, mean_table, edge


def dot(left, right):
    return jnp.dot(left, right, preferred_element_type=jnp.float32)


def split_dot(value, high, low):
    rows = value.shape[0]
    value_high = value.astype(jnp.bfloat16)
    value_low = (value - value_high.astype(jnp.float32)).astype(jnp.bfloat16)
    both = dot(jnp.concatenate([value_high, value_low], axis=0), high)
    return both[:rows] + both[rows:] + dot(value_high, low)


def start_tables(sources, places, arrivals):
    copies = [pltpu.make_async_copy(source, place, arrivals.at[at])
              for at, (source, place) in enumerate(zip(sources, places))]
    for copy in copies:
        copy.start()
    return copies


def band_rows(taps):
    rows = jnp.concatenate([taps, jnp.zeros((1, REACH - TAPS), jnp.float32)], axis=1)
    rows = jnp.broadcast_to(rows, (BLOCK, REACH))
    row_at = lax.broadcasted_iota(jnp.int32, (BLOCK, REACH), 0)
    step = 1
    while step < BLOCK:
        rows = jnp.where(row_at // step % 2 == 1, pltpu.roll(rows, step * DECIM, 1), rows)
        step *= 2
    return rows.astype(jnp.bfloat16)


def whiten_pair_kernel(windows, starts, live, strain, taps, *refs):
    sources, out, record = refs[:6], refs[6], refs[7]
    places, (arrivals, sent, landed) = refs[8:14], refs[14:]
    copies = start_tables(sources, places, arrivals)
    win_at = lax.axis_index("win")
    partner = (1 - win_at, lax.axis_index("chan"))
    barrier = pltpu.get_barrier_semaphore()
    pl.semaphore_signal(barrier, inc=1, device_id=partner, device_id_type=pl.DeviceIdType.MESH)
    pl.semaphore_wait(barrier, 1)
    swap = pltpu.make_async_remote_copy(
        src_ref=strain,
        dst_ref=record.at[win_at],
        send_sem=sent,
        recv_sem=landed,
        device_id=partner,
        device_id_type=pl.DeviceIdType.MESH,
    )
    swap.start()
    record[win_at] = strain[...]
    band = band_rows(taps[...])
    swap.wait()
    wide = jnp.concatenate([record[0].astype(jnp.float32), record[1].astype(jnp.float32)], axis=1)
    for copy in copies:
        copy.wait()
    whiten_rows(windows, starts, live, wide, band, places, out)


def whiten_all_kernel(windows, starts, live, record, taps, *refs):
    sources, out, places, arrivals = refs[:6], refs[6], refs[7:13], refs[13]
    copies = start_tables(sources, places, arrivals)
    band = band_rows(taps[...])
    wide = record[...].astype(jnp.float32)
    for copy in copies:
        copy.wait()
    whiten_rows(windows, starts, live, wide, band, places, out)


def whiten_rows(windows, starts, live, wide, band, places, out):
    forward_high, forward_low, inverse_high, inverse_low, mean_table, edge = places
    channels, length = wide.shape
    pieces = []
    for window_at in range(windows):
        start = starts[window_at]
        rolled = pltpu.roll(wide, lax.rem(length - start, length), 1).astype(jnp.bfloat16)
        parts = [
            lax.dot_general(
                rolled[:, at * BLOCK * DECIM : at * BLOCK * DECIM + REACH],
                band,
                (((1,), (1,)), ((), ())),
                preferred_element_type=jnp.float32,
            )
            for at in range(NS // BLOCK)
        ]
        pieces.append(jnp.concatenate(parts, axis=1))
    decimated = jnp.concatenate(pieces, axis=0)
    row_at = lax.broadcasted_iota(jnp.int32, (channels, NS), 0)
    kept = jnp.zeros((channels, NS), jnp.float32)
    for channel in range(channels):
        kept = jnp.where(row_at == channel, live[channel].astype(jnp.float32), kept)
    first, second = decimated[:, :FOLD], decimated[:, FOLD:]
    even = split_dot(first + second, forward_high[0], forward_low[0])
    odd = split_dot(first - second, forward_high[1], forward_low[1])
    quarter = NS // 4
    real_part = jnp.concatenate([even[:, :quarter], odd[:, :quarter]], axis=1)
    imag_part = jnp.concatenate([even[:, quarter:], odd[:, quarter:]], axis=1)
    at_zero = lax.broadcasted_iota(jnp.int32, real_part.shape, 1) == 0
    amplitude = jnp.sqrt(real_part * real_part + jnp.where(at_zero, 0.0, imag_part * imag_part))
    top = jnp.abs(imag_part[:, 0:1])
    amp_high = amplitude.astype(jnp.bfloat16)
    amp_low = (amplitude - amp_high.astype(jnp.float32)).astype(jnp.bfloat16)
    summed = dot(amp_high, mean_table[...]) + dot(amp_low, mean_table[...]) + top * edge[0:1, :]
    summed_top = jnp.sum(amplitude * edge[1:2, :], axis=1, keepdims=True) + top
    width = 2 * HALF + 1
    scale = 1.0 / (summed * (1.0 / width) + EPSILON)
    scale_top = 1.0 / (summed_top * (1.0 / width) + EPSILON)
    white_real = real_part * scale
    white_imag = imag_part * jnp.where(at_zero, scale_top, scale)
    white_even = jnp.concatenate([white_real[:, :quarter], white_imag[:, :quarter]], axis=1)
    white_odd = jnp.concatenate([white_real[:, quarter:], white_imag[:, quarter:]], axis=1)
    from_even = split_dot(white_even, inverse_high[0], inverse_low[0])
    from_odd = split_dot(white_odd, inverse_high[1], inverse_low[1])
    series = jnp.concatenate([from_even + from_odd, from_even - from_odd], axis=1)
    for window_at in range(windows):
        rows = series[window_at * channels : (window_at + 1) * channels]
        out[window_at] = (rows * kept).astype(jnp.bfloat16)


def lag_sums(place, gathered, turned, lagged):
    blocks, windows, channels, _ = gathered.shape
    sources = channels // STRIDE
    chan_at = place[1]
    source_block = chan_at // STRIDE * STRIDE
    source_part = lax.rem(chan_at, STRIDE)
    total = None
    for window_at in range(windows):
        rows = gathered[source_block, window_at].astype(jnp.float32)
        chosen = jnp.where(source_part == 0, rows[:sources], rows[sources:])
        for row in range(8):
            turned[:, row, :] = pltpu.roll(chosen, (NS - row) % NS, 1)
        for source in range(sources):
            base = turned[source]
            for first in range(0, LAG_ROWS, 16):
                pair = [pltpu.roll(base, (LAGS // 2 - first - 8 * at) % NS, 1) for at in range(2)]
                lagged[source, first : first + 16, :] = jnp.concatenate(pair, axis=0).astype(jnp.bfloat16)
        term = lax.dot_general(
            lagged[...].reshape(sources * LAG_ROWS, NS),
            gathered[:, window_at].reshape(blocks * channels, NS),
            (((1,), (1,)), ((), ())),
            preferred_element_type=jnp.float32,
        )
        total = term if total is None else total + term
    return total


def gather_corr_kernel(scale, series, out, held, turned, lagged, outgoing, arrived,
                       sent, landed, swap_sent, swap_landed):
    blocks, windows, channels, _ = held.shape
    sources = channels // STRIDE
    layers = blocks // 4
    win_at = lax.axis_index("win")
    me = lax.axis_index("chan")
    layer, core = me // 4, lax.rem(me, 2)
    lane = lax.rem(me, 4)
    beside = layer * 4 + lax.rem(lane + 2, 4)
    twin = me + 1 - 2 * core
    twin_lane = lane + 1 - 2 * core
    other_lane = lax.rem(lane + 2, 4)
    partner = 1 - win_at
    above, below = me + 4, me - 4
    has_above, has_below = layer < layers - 1, layer > 0
    mesh_id = pl.DeviceIdType.MESH

    barrier = pltpu.get_barrier_semaphore()
    pl.semaphore_signal(barrier, inc=1, device_id=(win_at, beside), device_id_type=mesh_id)
    pl.semaphore_signal(barrier, inc=1, device_id=(win_at, twin), device_id_type=mesh_id)
    pl.semaphore_signal(barrier, inc=1, device_id=(partner, me), device_id_type=mesh_id)

    @pl.when(has_above)
    def _():
        pl.semaphore_signal(barrier, inc=1, device_id=(win_at, above), device_id_type=mesh_id)

    @pl.when(has_below)
    def _():
        pl.semaphore_signal(barrier, inc=1, device_id=(win_at, below), device_id_type=mesh_id)

    held[me] = series[...]
    pl.semaphore_wait(barrier, 3 + has_above.astype(jnp.int32) + has_below.astype(jnp.int32))

    chunk = windows // CHUNKS

    def move(way, block, part, target):
        span = held.at[block, pl.ds(part * chunk, chunk)]
        return pltpu.make_async_remote_copy(
            src_ref=span,
            dst_ref=span,
            send_sem=sent.at[way, block, part],
            recv_sem=landed.at[block, part],
            device_id=(win_at, target),
            device_id_type=mesh_id,
        )

    def up(block, part):
        return move(0, block, part, above)

    def down(block, part):
        return move(1, block, part, below)

    def across(block, part):
        return move(2, block, part, beside)

    def over(block, part):
        return move(3, block, part, twin)

    def await_block(block, part):
        across(block, part).wait_recv()

    def when(condition, action):
        @pl.when(condition)
        def _():
            action()

    for part in range(CHUNKS):
        when(has_above, lambda: up(me, part).start())
        when(has_below, lambda: down(me, part).start())
        across(me, part).start()
        over(me, part).start()

    source_block = me // STRIDE * STRIDE
    source_part = lax.rem(me, STRIDE)

    def build(window_at):
        rows = held[source_block, window_at].astype(jnp.float32)
        chosen = jnp.where(source_part == 0, rows[:sources], rows[sources:])
        for row in range(8):
            turned[:, row, :] = pltpu.roll(chosen, (NS - row) % NS, 1)

        def build_source(source, carry):
            base = turned[source]
            for first in range(0, LAG_ROWS, 16):
                pair = [pltpu.roll(base, (LAGS // 2 - first - 8 * at) % NS, 1) for at in range(2)]
                lagged[window_at, source, first : first + 16, :] = jnp.concatenate(pair, axis=0).astype(jnp.bfloat16)
            return carry

        lax.fori_loop(0, sources, build_source, 0)

    def pass_lane(distance, part):
        for sign in (-1, 1):
            origin = layer + sign * distance
            block = me + 4 * sign * distance
            exists = (origin >= 0) if sign < 0 else (origin < layers)
            further = has_above if sign < 0 else has_below

            def relay():
                await_block(block, part)
                when(further, lambda: (up if sign < 0 else down)(block, part).start())
                across(block, part).start()
                over(block, part).start()

            when(exists, relay)

    def pass_beside(distance, part):
        for sign in (-1, 1) if distance else (1,):
            origin = layer + sign * distance
            block = origin * 4 + other_lane
            exists = (origin >= 0) if sign < 0 else (origin < layers)

            def relay():
                await_block(block, part)
                over(block, part).start()

            when(exists, relay)

    to_build = list(range(windows))
    for part in range(CHUNKS):
        await_block(twin, part)
    build(to_build.pop(0))
    for distance in range(1, layers):
        for part in range(CHUNKS):
            pass_lane(distance, part)
            if to_build:
                build(to_build.pop(0))
            pass_beside(distance - 1, part)
    while to_build:
        build(to_build.pop(0))
    half_blocks = blocks // 2

    def window_sums(half, window_at):
        return lax.dot_general(
            lagged[window_at].reshape(sources * LAG_ROWS, NS),
            held[pl.ds(half * half_blocks, half_blocks), window_at].reshape(half_blocks * channels, NS),
            (((1,), (1,)), ((), ())),
            preferred_element_type=jnp.float32,
        )

    for part in range(CHUNKS):
        pass_beside(layers - 1, part)
    partial = None
    for part in range(CHUNKS):
        for at in range(layers):
            await_block(at * 4 + lax.rem(twin_lane + 2, 4), part)
            mine = at * 4 + twin_lane
            when(mine != twin, lambda: await_block(mine, part))
        for window_at in range(part * chunk, (part + 1) * chunk):
            term = window_sums(partner, window_at)
            partial = term if partial is None else partial + term

    def own_sums():
        total = None
        for window_at in range(windows):
            term = window_sums(win_at, window_at)
            total = term if total is None else total + term
        return total * scale

    outgoing[...] = (partial * scale).astype(jnp.bfloat16).reshape(outgoing.shape)
    swap = pltpu.make_async_remote_copy(
        src_ref=outgoing,
        dst_ref=arrived,
        send_sem=swap_sent,
        recv_sem=swap_landed,
        device_id=(partner, me),
        device_id_type=mesh_id,
    )
    swap.start()
    kept = own_sums().reshape(outgoing.shape)
    swap.wait()
    total = kept + arrived[...].astype(jnp.float32)
    for source in range(sources):
        out[source] = total[source, :LAGS]

    for at in range(layers):
        block = at * 4 + lane
        for part in range(CHUNKS):
            when(jnp.logical_and(has_above, at <= layer), lambda: up(block, part).wait_send())
            when(jnp.logical_and(has_below, at >= layer), lambda: down(block, part).wait_send())
            across(block, part).wait_send()
            over(block, part).wait_send()
            over(at * 4 + other_lane, part).wait_send()


def corr_all_kernel(scale, place, gathered, own, turned, lagged):
    total = lag_sums(place, gathered, turned, lagged) * scale
    for source in range(own.shape[0]):
        own[source] = total[source * LAG_ROWS : source * LAG_ROWS + LAGS]


def whole_in_vmem(count):
    return [pl.BlockSpec(memory_space=pltpu.VMEM)] * count


def local(tables, strain_raw, fir_taps, live_mask, window_start):
    channels = strain_raw.shape[0]
    windows = window_start.shape[0]
    groups = lax.axis_size("win")
    blocks = lax.axis_size("chan")
    win_at = lax.axis_index("win")
    chan_at = lax.axis_index("chan")
    params = pltpu.CompilerParams(vmem_limit_bytes=VMEM_LIMIT)
    smem = pl.BlockSpec(memory_space=pltpu.SMEM)
    places = [pltpu.VMEM(table.shape, table.dtype) for table in tables]
    taps = fir_taps.astype(jnp.float32)[None, :]
    whiten_specs = dict(
        out_shape=jax.ShapeDtypeStruct((windows, channels, NS), jnp.bfloat16),
        in_specs=[smem, smem] + whole_in_vmem(2) + [pl.BlockSpec(memory_space=pltpu.HBM)] * len(tables),
        out_specs=pl.BlockSpec(memory_space=pltpu.VMEM),
        name="whiten",
    )
    if groups == 2:
        series = pl.pallas_call(
            lambda *refs: whiten_pair_kernel(windows, *refs),
            scratch_shapes=[pltpu.VMEM((2,) + strain_raw.shape, strain_raw.dtype)]
            + places
            + [pltpu.SemaphoreType.DMA((len(tables),)), pltpu.SemaphoreType.DMA, pltpu.SemaphoreType.DMA],
            compiler_params=pltpu.CompilerParams(
                vmem_limit_bytes=VMEM_LIMIT, collective_id=1, has_side_effects=True
            ),
            **whiten_specs,
        )(window_start, live_mask, strain_raw, taps, *tables)
    else:
        record = lax.all_gather(strain_raw, "win", axis=1, tiled=True)
        series = pl.pallas_call(
            lambda *refs: whiten_all_kernel(windows, *refs),
            scratch_shapes=places + [pltpu.SemaphoreType.DMA((len(tables),))],
            compiler_params=params,
            **whiten_specs,
        )(window_start, live_mask, record, taps, *tables)
    scale = 1.0 / (math.sqrt(NS) * math.sqrt(windows * groups))
    sources = channels // STRIDE
    total = blocks * channels
    if groups == 2 and blocks == 16:
        return pl.pallas_call(
            lambda *refs: gather_corr_kernel(scale, *refs),
            out_shape=jax.ShapeDtypeStruct((sources, LAGS, total // 2), jnp.float32),
            in_specs=whole_in_vmem(1),
            out_specs=pl.BlockSpec(memory_space=pltpu.VMEM),
            scratch_shapes=[
                pltpu.VMEM((blocks, windows, channels, NS), jnp.bfloat16),
                pltpu.VMEM((sources, 8, NS), jnp.float32),
                pltpu.VMEM((windows, sources, LAG_ROWS, NS), jnp.bfloat16),
                pltpu.VMEM((sources, LAG_ROWS, total // 2), jnp.bfloat16),
                pltpu.VMEM((sources, LAG_ROWS, total // 2), jnp.bfloat16),
                pltpu.SemaphoreType.DMA((4, blocks, CHUNKS)),
                pltpu.SemaphoreType.DMA((blocks, CHUNKS)),
                pltpu.SemaphoreType.DMA,
                pltpu.SemaphoreType.DMA,
            ],
            compiler_params=pltpu.CompilerParams(
                vmem_limit_bytes=CORR_VMEM_LIMIT, collective_id=0, has_side_effects=True
            ),
            name="gather_correlate",
        )(series)
    gathered = lax.all_gather(series, "chan", axis=0, tiled=False)
    place = jnp.stack([win_at, chan_at]).astype(jnp.int32)
    scratch = [
        pltpu.VMEM((sources, 8, NS), jnp.float32),
        pltpu.VMEM((sources, LAG_ROWS, NS), jnp.bfloat16),
    ]
    own = pl.pallas_call(
        lambda *refs: corr_all_kernel(scale, *refs),
        out_shape=jax.ShapeDtypeStruct((sources, LAGS, total), jnp.float32),
        in_specs=[smem] + whole_in_vmem(1),
        out_specs=pl.BlockSpec(memory_space=pltpu.VMEM),
        scratch_shapes=scratch,
        compiler_params=params,
        name="correlate",
    )(place, gathered)
    return lax.psum_scatter(own, "win", scatter_dimension=2, tiled=True)


def solution(mesh):
    in_specs = (P("chan", "win"), P(), P("chan"), P("win"))
    out_specs = P("chan", None, "win")

    def run(strain_raw, fir_taps, live_mask, window_start):
        tables = [jnp.asarray(table) for table in build_tables()]
        mapped = jax.shard_map(
            lambda tables, *args: local(tables, *args),
            mesh=mesh,
            in_specs=(P(),) + in_specs,
            out_specs=out_specs,
            check_vma=False,
        )
        return mapped(tables, strain_raw, fir_taps, live_mask, window_start)

    return run
```
